256 devices in a mesh: occ: 64 (over y_lo, z, x), vir: 4 (over y_hi, core).
Axes of the slice: x: 4, y: 4 (y_hi: 2, y_lo: 2; y = y_hi * 2 + y_lo), z: 8, core: 2. Of those that a mesh axis runs over, the one named last changes fastest.
Arguments:
- amplitudes: float32 [32768, 2048], P('occ', 'vir'), may hold values from -6 to 6
- integrals: float32 [2048, 8192], P('vir', 'occ'), may hold values from -0.375 to 0.375
- ij_irrep: int32 [32768], P('occ'), may hold values from 0 to 7
- cd_irrep: int32 [2048], P('vir'), may hold values from 0 to 7
- ab_irrep: int32 [8192], P('occ'), may hold values from 0 to 7
Outputs:
- ladder: float32 [32768, 8192], P('occ', 'vir')
The draws below stay inside these ranges and needn't reach their ends.
All inputs are finite; a program needn't handle non-finite values.
Results may differ from the reference program's by a relative error of at most 0.0003.
Values sent between devices are 32-bit elements; how exact they have to be, the bound alone decides.
A program may use at most 128 MiB of HBM per device.

```python
import jax
import jax.numpy as jnp
from jax import lax

CD = 2048
AB = 8192
IRREPS = 8
IJ_DEV = 512
PAIRS = 32768
N_OCC = 64


def plant(result, own_key, low, top_value):
    place = [jax.random.randint(jax.random.fold_in(own_key, axis), (), 0, length) for axis, length in enumerate(result.shape)]
    widest = result.shape.index(max(result.shape))
    beside = place[:widest] + [(place[widest] + 1) % result.shape[widest]] + place[widest + 1:]
    return result.at[tuple(place)].set(low).at[tuple(beside)].set(top_value)


def block_scale(own_key, dims, split, low, high):
    level = 1.0
    for dim, shards_of in split:
        draws = jax.random.uniform(jax.random.fold_in(jax.random.fold_in(own_key, 6), dim), (shards_of,), jnp.float32, low / len(split), high / len(split))
        level = level * jnp.repeat(jnp.exp(draws), dims[dim] // shards_of).reshape((-1,) + (1,) * (len(dims) - 1 - dim))
    return level


def gaussian(key, extent, deviation, bound, cuts=(), held_as=jnp.bfloat16):
    entries = deviation * jax.random.normal(key, extent, jnp.float32)
    if cuts:
        entries = entries * block_scale(key, extent, cuts, -0.22, 0.18)
    return jnp.clip(entries, -bound, bound).astype(held_as)


def setup_inputs(seed: int = 0) -> dict:
    arg_keys = jax.random.split(jax.random.key(seed), 6)
    return {
        "amplitudes": gaussian(arg_keys[0], (PAIRS, CD), 1.0, 6.0, ((0, 64), (1, 4)), jnp.float32),
        "integrals": gaussian(arg_keys[1], (CD, AB), (CD // IRREPS) ** -0.5, 0.375, ((0, 4), (1, 64)), jnp.float32),
        "ij_irrep": plant(jax.random.randint(arg_keys[2], (PAIRS,), 0, IRREPS), jax.random.fold_in(arg_keys[2], 1), 0, IRREPS - 1).astype(jnp.int32),
        "cd_irrep": plant(jax.random.randint(arg_keys[3], (CD,), 0, IRREPS), jax.random.fold_in(arg_keys[3], 1), 0, IRREPS - 1).astype(jnp.int32),
        "ab_irrep": plant(jax.random.randint(arg_keys[4], (AB,), 0, IRREPS), jax.random.fold_in(arg_keys[4], 1), 0, IRREPS - 1).astype(jnp.int32),
    }


def reference(amplitudes, integrals, ij_irrep, cd_irrep, ab_irrep):
    v_sym = jnp.where(cd_irrep[:, None] == ab_irrep[None, :], integrals, jnp.float32(0.0))
    rows = amplitudes.reshape(N_OCC, IJ_DEV, CD)
    labels = ij_irrep.reshape(N_OCC, IJ_DEV)

    def one_block(pair):
        block, label = pair
        t_sym = jnp.where(label[:, None] == cd_irrep[None, :], block, jnp.float32(0.0))
        return jnp.dot(t_sym, v_sym, preferred_element_type=jnp.float32, precision=lax.Precision.HIGHEST)

    ladder = lax.map(one_block, (rows, labels))
    return ladder.reshape(PAIRS, AB)
```

```python
import functools

import jax
import jax.numpy as jnp
from jax import lax
from jax.experimental import pallas as pl
from jax.experimental.pallas import tpu as pltpu
from jax.sharding import PartitionSpec as P

MESH = pl.DeviceIdType.MESH
G = 8
CAP = 95
ROWS = CAP + 1
NX, NZ = 4, 8
F32, BF16 = jnp.float32, jnp.bfloat16


def split(value):
    high = value.astype(BF16)
    return high, (value - high.astype(F32)).astype(BF16)


def compact_kernel(round_ref, t_ref, v_ref, ij_ref, cd_ref, ab_ref, tc_ref, vc_ref):
    n_cd = cd_ref.shape[1]
    labels = cd_ref[...]
    member = lax.broadcasted_iota(jnp.int32, (G, n_cd), 0) == labels
    before = lax.broadcasted_iota(jnp.int32, (n_cd, n_cd), 0) < lax.broadcasted_iota(
        jnp.int32, (n_cd, n_cd), 1
    )
    below = jnp.dot(member.astype(BF16), before.astype(BF16), preferred_element_type=F32)
    rank = jnp.sum(jnp.where(member, below, 0.0), axis=0, keepdims=True).astype(jnp.int32)
    most = jnp.max(jnp.sum(member.astype(F32), axis=1, keepdims=True), axis=0, keepdims=True)
    place = rank - CAP * round_ref[0, 0]
    slot = jnp.where((place >= 0) & (place < CAP), labels * ROWS + place, -1)
    pick = (lax.broadcasted_iota(jnp.int32, (G * ROWS, n_cd), 0) == slot).astype(BF16)
    pick2 = jnp.concatenate([pick, pick], axis=1)

    def compacted(both, dims, column_labels, last_row):
        wide = lax.dot_general(pick2, both, (dims, ((), ())), preferred_element_type=F32)
        out = jnp.zeros((ROWS, wide.shape[1]), F32)
        for g in range(G):
            out = jnp.where(column_labels == g, wide[g * ROWS : (g + 1) * ROWS], out)
        row = lax.broadcasted_iota(jnp.int32, out.shape, 0)
        return jnp.where(row == CAP, last_row, out)

    ab = ab_ref[...]
    vc_ref[...] = compacted(
        jnp.concatenate(split(v_ref[...]), axis=0), ((1,), (0,)), ab, ab.astype(F32)
    )
    tc_ref[...] = compacted(
        jnp.concatenate(split(t_ref[...]), axis=1), ((1,), (1,)), ij_ref[...], most
    )


def compact(round_index, t, v, ij, cd, ab):
    vmem = pl.BlockSpec(memory_space=pltpu.VMEM)
    return pl.pallas_call(
        compact_kernel,
        out_shape=(
            jax.ShapeDtypeStruct((ROWS, t.shape[0]), F32),
            jax.ShapeDtypeStruct((ROWS, v.shape[1]), F32),
        ),
        in_specs=[pl.BlockSpec(memory_space=pltpu.SMEM)] + [vmem] * 5,
        out_specs=(vmem, vmem),
        compiler_params=pltpu.CompilerParams(vmem_limit_bytes=32 << 20),
        name="compact",
    )(round_index, t, v, ij[None, :], cd[None, :], ab[None, :])


def z_sends(quarter, d):
    up, down = (4, 3) if quarter % 2 == 0 else (3, 4)
    out = []
    if d < up:
        out.append(1)
    if d == 0 or 8 - d < down:
        out.append(-1)
    if d and d <= up and 8 - d <= down:
        raise ValueError
    if 0 < d <= up:
        return [s for s in out if s == 1]
    if d:
        return [s for s in out if s == -1]
    return out


def x_sends(quarter, dx):
    if dx == 0:
        return [1, -1]
    if dx == 1 and quarter % 2 == 0:
        return [1]
    if dx == 3 and quarter % 2 == 1:
        return [-1]
    return []


def gather_events():
    events = []
    for quarter in range(4):
        for d in range(8):
            for dx in range(4):
                x_hops = min(dx, 4 - dx)
                z_hops = min(d, 8 - d)
                if quarter < 2:
                    xs = x_sends(quarter, dx) if d == 0 else []
                    zs = z_sends(quarter, d)
                else:
                    xs = x_sends(quarter, dx)
                    zs = z_sends(quarter, d) if dx == 0 else []
                when = x_hops + z_hops
                events.append((when, z_hops if quarter < 2 else x_hops, quarter, d, dx, xs, zs))
    events.sort(key=lambda e: (e[0], e[1], e[3], e[4], e[2]))
    return [e[2:] for e in events]


EVENTS = gather_events()
N_SENDS = sum(len(e[3]) + len(e[4]) for e in EVENTS)


def gather_kernel(tc_ref, vc_ref, tg_ref, vg_ref, v_send, v_recv, y_send, t_send, t_recv, own_sem):
    occ, vir = lax.axis_index("occ"), lax.axis_index("vir")
    y_lo, z, x = occ // (NX * NZ), (occ // NX) % NZ, occ % NX
    y_hi, core = vir // 2, vir % 2
    u = (z + NZ - 4 * core) % NZ

    def at(y, z, x):
        return y * (NX * NZ) + z * NX + x

    def near_x(step):
        return (at(y_lo, z, (x + NX + step) % NX), vir)

    def near_z(step):
        return (at(y_lo, (z + NZ + step) % NZ, x), vir)

    other_y = (1 - y_lo) * (NX * NZ) + z * NX + x
    barrier = pltpu.get_barrier_semaphore()
    peers = [near_x(1), near_x(-1), near_z(1), near_z(-1)]
    peers += [(occ, (vir + k) % 4) for k in range(1, 4)]
    peers += [(other_y, k) for k in range(4)]
    for peer in peers:
        pl.semaphore_signal(barrier, inc=1, device_id=peer, device_id_type=MESH)
    pl.semaphore_wait(barrier, len(peers))

    block = (z % 4) * NX + x
    for k in range(2):
        target = (at(k, z, x), 2 * y_lo + z // 4)
        mine = (y_lo == k) & (vir == 2 * y_lo + z // 4)

        @pl.when(mine)
        def _():
            pltpu.make_async_copy(
                vc_ref, vg_ref.at[block, vir], v_recv.at[block * 4 + vir]
            ).start()

        @pl.when(jnp.logical_not(mine))
        def _():
            pltpu.make_async_remote_copy(
                src_ref=vc_ref,
                dst_ref=vg_ref.at[block, vir],
                send_sem=y_send.at[k],
                recv_sem=v_recv.at[block * 4 + vir],
                device_id=target,
                device_id_type=MESH,
            ).start()

    def t_copy(k):
        return pltpu.make_async_remote_copy(
            src_ref=tc_ref,
            dst_ref=tg_ref.at[vir],
            send_sem=t_send.at[k - 1],
            recv_sem=t_recv.at[k - 1],
            device_id=(occ, (vir + k) % 4),
            device_id_type=MESH,
        )

    own = pltpu.make_async_copy(tc_ref, tg_ref.at[vir], own_sem)

    def v_copy(quarter, zl, xs, peer, sem):
        here = vg_ref.at[zl * NX + xs, quarter]
        return pltpu.make_async_remote_copy(
            src_ref=here,
            dst_ref=here,
            send_sem=v_send.at[sem],
            recv_sem=v_recv.at[(zl * NX + xs) * 4 + quarter],
            device_id=peer,
            device_id_type=MESH,
        )

    def walk(act):
        sem = 0
        for quarter, d, dx, x_dirs, z_dirs in EVENTS:
            zl = (u + 8 - d) % 8
            xs = (x + NX - dx) % NX
            peers = [near_x(s) for s in x_dirs] + [near_z(s) for s in z_dirs]
            first = sem
            sem += len(peers)

            @pl.when(zl < 4)
            def _():
                act(quarter, zl, xs, peers, first)

    def receive_and_pass(quarter, zl, xs, peers, first):
        here = vg_ref.at[zl * NX + xs, quarter]
        pltpu.make_async_copy(here, here, v_recv.at[(zl * NX + xs) * 4 + quarter]).wait()
        for i, peer in enumerate(peers):
            v_copy(quarter, zl, xs, peer, first + i).start()

    def finish(quarter, zl, xs, peers, first):
        for i, peer in enumerate(peers):
            v_copy(quarter, zl, xs, peer, first + i).wait_send()

    own.start()
    for k in range(1, 4):
        t_copy(k).start()
    walk(receive_and_pass)
    walk(finish)
    own.wait()
    for k in range(1, 4):
        t_copy(k).wait()
    for k in range(2):
        mine = (y_lo == k) & (vir == 2 * y_lo + z // 4)

        @pl.when(jnp.logical_not(mine))
        def _():
            pltpu.make_async_remote_copy(
                src_ref=vc_ref,
                dst_ref=vg_ref.at[block, vir],
                send_sem=y_send.at[k],
                recv_sem=v_recv.at[block * 4 + vir],
                device_id=(at(k, z, x), 2 * y_lo + z // 4),
                device_id_type=MESH,
            ).wait_send()


def gather(tc, vc):
    anywhere = pl.BlockSpec(memory_space=pl.ANY)
    return pl.pallas_call(
        gather_kernel,
        out_shape=(
            jax.ShapeDtypeStruct((4,) + tc.shape, F32),
            jax.ShapeDtypeStruct((16, 4) + vc.shape, F32),
        ),
        in_specs=[anywhere, anywhere],
        out_specs=(anywhere, anywhere),
        scratch_shapes=[
            pltpu.SemaphoreType.DMA((N_SENDS,)),
            pltpu.SemaphoreType.DMA((64,)),
            pltpu.SemaphoreType.DMA((2,)),
            pltpu.SemaphoreType.DMA((3,)),
            pltpu.SemaphoreType.DMA((3,)),
            pltpu.SemaphoreType.DMA,
        ],
        compiler_params=pltpu.CompilerParams(collective_id=0, has_side_effects=True),
        name="gather",
    )(tc, vc)


def product_kernel(tg_ref, vg_ref, ij_ref, out_ref, rounds_ref, left, mask_col):
    slabs = tg_ref.shape[0]

    @pl.when(pl.program_id(0) == 0)
    def _():
        most = jnp.int32(0)
        for s in range(slabs):
            most = jnp.maximum(most, jnp.max(tg_ref[s, CAP:ROWS, :]).astype(jnp.int32))
        rounds_ref[0, 0] = (most + (CAP - 1)) // CAP
        parts = []
        row = lax.broadcasted_iota(jnp.int32, (ROWS, tg_ref.shape[2]), 0)
        for s in range(slabs):
            parts.append(jnp.where(row == CAP, 0.0, tg_ref[s]))
        high, low = split(jnp.concatenate(parts, axis=0).T)
        left[...] = jnp.concatenate([high, high, low], axis=1)
        mask_col[...] = jnp.broadcast_to(ij_ref[...].astype(F32), (128, ij_ref.shape[1])).T

    blocks = vg_ref.shape[0]
    value = jnp.concatenate(
        [
            jnp.concatenate([vg_ref[b, s] for s in range(slabs)], axis=0)
            for b in range(blocks)
        ],
        axis=1,
    )
    labels = jnp.concatenate([vg_ref[b, 0, CAP:ROWS, :] for b in range(blocks)], axis=1)
    high, low = split(value)
    right = jnp.concatenate([high, low, high], axis=0)
    total = jnp.dot(left[...], right, preferred_element_type=F32)
    same = jnp.concatenate([mask_col[...]] * blocks, axis=1) == labels
    out_ref[...] = jnp.where(same, total, 0.0)


def product(tg, vg, ij):
    slabs, rows, n_ij = tg.shape
    per_step = 2
    return pl.pallas_call(
        product_kernel,
        out_shape=(
            jax.ShapeDtypeStruct((n_ij, vg.shape[0] * 128), F32),
            jax.ShapeDtypeStruct((1, 1), jnp.int32),
        ),
        grid=(vg.shape[0] // per_step,),
        in_specs=[
            pl.BlockSpec(tg.shape, lambda i: (0, 0, 0)),
            pl.BlockSpec((per_step,) + vg.shape[1:], lambda i: (i, 0, 0, 0)),
            pl.BlockSpec((1, n_ij), lambda i: (0, 0)),
        ],
        out_specs=(
            pl.BlockSpec((n_ij, per_step * 128), lambda i: (0, i)),
            pl.BlockSpec((1, 1), lambda i: (0, 0), memory_space=pltpu.SMEM),
        ),
        scratch_shapes=[
            pltpu.VMEM((n_ij, 3 * slabs * rows), BF16),
            pltpu.VMEM((n_ij, 128), F32),
        ],
        compiler_params=pltpu.CompilerParams(vmem_limit_bytes=32 << 20),
        name="product",
    )(tg, vg, ij[None, :])


def per_device(amplitudes, integrals, ij_irrep, cd_irrep, ab_irrep):
    args = (amplitudes, integrals, ij_irrep, cd_irrep, ab_irrep)
    tc, vc = compact(jnp.zeros((1, 1), jnp.int32), *args)
    tg, vg = gather(tc, vc)
    ladder, rounds = product(tg, vg, ij_irrep)

    def more(state):
        return state[0] < rounds[0, 0]

    def one_round(state):
        index, total = state
        tc, vc = compact(index.reshape(1, 1), *args)
        tg = lax.all_gather(tc, "vir", axis=0)
        vg = lax.all_gather(lax.all_gather(vc, "occ", axis=0), "vir", axis=1)
        vg = lax.dynamic_slice_in_dim(vg, 16 * lax.axis_index("vir"), 16, axis=0)
        return index + 1, total + product(tg, vg, ij_irrep)[0]

    return lax.while_loop(more, one_round, (jnp.int32(1), ladder))[1]


def solution(mesh):
    in_specs = (P("occ", "vir"), P("vir", "occ"), P("occ"), P("vir"), P("occ"))
    out_specs = P("occ", "vir")
    return jax.shard_map(
        per_device, mesh=mesh, in_specs=in_specs, out_specs=out_specs, check_vma=False
    )
```

```python
import functools

import jax
import jax.numpy as jnp
from jax import lax
from jax.experimental import pallas as pl
from jax.experimental.pallas import tpu as pltpu
from jax.sharding import PartitionSpec as P

MESH = pl.DeviceIdType.MESH
G = 8
CAP = 95
ROWS = CAP + 1
NX, NZ = 4, 8
F32, BF16 = jnp.float32, jnp.bfloat16


def split(value):
    high = value.astype(BF16)
    return high, (value - high.astype(F32)).astype(BF16)


def compact_kernel(round_ref, t_ref, v_ref, ij_ref, cd_ref, ab_ref, tc_ref, vc_ref):
    n_cd = cd_ref.shape[1]
    labels = cd_ref[...]
    member = lax.broadcasted_iota(jnp.int32, (G, n_cd), 0) == labels
    before = lax.broadcasted_iota(jnp.int32, (n_cd, n_cd), 0) < lax.broadcasted_iota(
        jnp.int32, (n_cd, n_cd), 1
    )
    below = jnp.dot(member.astype(BF16), before.astype(BF16), preferred_element_type=F32)
    rank = jnp.sum(jnp.where(member, below, 0.0), axis=0, keepdims=True).astype(jnp.int32)
    most = jnp.max(jnp.sum(member.astype(F32), axis=1, keepdims=True), axis=0, keepdims=True)
    place = rank - CAP * round_ref[0, 0]
    slot = jnp.where((place >= 0) & (place < CAP), labels * ROWS + place, -1)
    pick = (lax.broadcasted_iota(jnp.int32, (G * ROWS, n_cd), 0) == slot).astype(BF16)
    pick2 = jnp.concatenate([pick, pick], axis=1)

    def compacted(both, dims, column_labels, last_row):
        wide = lax.dot_general(pick2, both, (dims, ((), ())), preferred_element_type=F32)
        out = jnp.zeros((ROWS, wide.shape[1]), F32)
        for g in range(G):
            out = jnp.where(column_labels == g, wide[g * ROWS : (g + 1) * ROWS], out)
        row = lax.broadcasted_iota(jnp.int32, out.shape, 0)
        return jnp.where(row == CAP, last_row, out)

    ab = ab_ref[...]
    vc_ref[...] = compacted(
        jnp.concatenate(split(v_ref[...]), axis=0), ((1,), (0,)), ab, ab.astype(F32)
    )
    tc_ref[...] = compacted(
        jnp.concatenate(split(t_ref[...]), axis=1), ((1,), (1,)), ij_ref[...], most
    )


def compact(round_index, t, v, ij, cd, ab):
    vmem = pl.BlockSpec(memory_space=pltpu.VMEM)
    return pl.pallas_call(
        compact_kernel,
        out_shape=(
            jax.ShapeDtypeStruct((ROWS, t.shape[0]), F32),
            jax.ShapeDtypeStruct((ROWS, v.shape[1]), F32),
        ),
        in_specs=[pl.BlockSpec(memory_space=pltpu.SMEM)] + [vmem] * 5,
        out_specs=(vmem, vmem),
        compiler_params=pltpu.CompilerParams(vmem_limit_bytes=32 << 20),
        name="compact",
    )(round_index, t, v, ij[None, :], cd[None, :], ab[None, :])


def z_sends(quarter, d):
    up, down = (4, 3) if quarter % 2 == 0 else (3, 4)
    out = []
    if d < up:
        out.append(1)
    if d == 0 or 8 - d < down:
        out.append(-1)
    if d and d <= up and 8 - d <= down:
        raise ValueError
    if 0 < d <= up:
        return [s for s in out if s == 1]
    if d:
        return [s for s in out if s == -1]
    return out


def x_sends(quarter, dx):
    if dx == 0:
        return [1, -1]
    if dx == 1 and quarter % 2 == 0:
        return [1]
    if dx == 3 and quarter % 2 == 1:
        return [-1]
    return []


def gather_events():
    events = []
    for quarter in range(4):
        for d in range(8):
            for dx in range(4):
                x_hops = min(dx, 4 - dx)
                z_hops = min(d, 8 - d)
                if quarter < 2:
                    xs = x_sends(quarter, dx) if d == 0 else []
                    zs = z_sends(quarter, d)
                else:
                    xs = x_sends(quarter, dx)
                    zs = z_sends(quarter, d) if dx == 0 else []
                when = x_hops + z_hops
                events.append((when, z_hops if quarter < 2 else x_hops, quarter, d, dx, xs, zs))
    events.sort(key=lambda e: (e[0], e[1], e[3], e[4], e[2]))
    return [e[2:] for e in events]


EVENTS = gather_events()
N_SENDS = sum(len(e[3]) + len(e[4]) for e in EVENTS)


def gather_kernel(tc_ref, vc_ref, tg_ref, vg_ref, v_send, v_recv, y_send, t_send, t_recv, own_sem):
    occ, vir = lax.axis_index("occ"), lax.axis_index("vir")
    y_lo, z, x = occ // (NX * NZ), (occ // NX) % NZ, occ % NX
    y_hi, core = vir // 2, vir % 2
    u = (z + NZ - 4 * core) % NZ

    def at(y, z, x):
        return y * (NX * NZ) + z * NX + x

    def near_x(step):
        return (at(y_lo, z, (x + NX + step) % NX), vir)

    def near_z(step):
        return (at(y_lo, (z + NZ + step) % NZ, x), vir)

    owner = z // 4 == core
    mine = owner & (y_lo == y_hi)
    sibling, across = (occ, vir + 1 - 2 * core), (occ, (vir + 2) % 4)

    barrier = pltpu.get_barrier_semaphore()

    def ready_for(peer):
        pl.semaphore_signal(barrier, inc=1, device_id=peer, device_id_type=MESH)

    for peer in (near_x(1), near_x(-1), sibling, across):
        ready_for(peer)
    pl.when(u != 0)(lambda: ready_for(near_z(-1)))
    pl.when(u != 3)(lambda: ready_for(near_z(1)))
    for k in range(4):
        pl.when(owner & jnp.logical_not(mine & (vir == k)))(
            lambda: ready_for((at(y_hi, z, x), k))
        )
    heard = 6 + (u != 7).astype(jnp.int32) + (u != 4).astype(jnp.int32)
    pl.semaphore_wait(barrier, heard - mine.astype(jnp.int32))

    block = (z % 4) * NX + x
    for k in range(2):
        target = (at(k, z, x), 2 * y_lo + z // 4)
        here = mine & (y_lo == k)

        @pl.when(here)
        def _():
            pltpu.make_async_copy(
                vc_ref, vg_ref.at[block, vir], v_recv.at[block * 4 + vir]
            ).start()

        @pl.when(jnp.logical_not(here))
        def _():
            pltpu.make_async_remote_copy(
                src_ref=vc_ref,
                dst_ref=vg_ref.at[block, vir],
                send_sem=y_send.at[k],
                recv_sem=v_recv.at[block * 4 + vir],
                device_id=target,
                device_id_type=MESH,
            ).start()

    def t_copy(k, src, slab, peer):
        return pltpu.make_async_remote_copy(
            src_ref=src,
            dst_ref=tg_ref.at[slab],
            send_sem=t_send.at[k],
            recv_sem=t_recv.at[k],
            device_id=peer,
            device_id_type=MESH,
        )

    far = (vir + 2) % 4
    t_across = t_copy(0, tc_ref, vir, across)
    t_near = t_copy(1, tc_ref, vir, sibling)
    t_pass = t_copy(2, tg_ref.at[far], far, sibling)
    own = pltpu.make_async_copy(tc_ref, tg_ref.at[vir], own_sem)

    def v_copy(quarter, zl, xs, peer, sem):
        here = vg_ref.at[zl * NX + xs, quarter]
        return pltpu.make_async_remote_copy(
            src_ref=here,
            dst_ref=here,
            send_sem=v_send.at[sem],
            recv_sem=v_recv.at[(zl * NX + xs) * 4 + quarter],
            device_id=peer,
            device_id_type=MESH,
        )

    def walk(act):
        sem = 0
        for n, (quarter, d, dx, x_dirs, z_dirs) in enumerate(EVENTS):
            if n == len(EVENTS) // 3 and act is receive_and_pass:
                t_across.wait_recv()
                t_pass.start()
            zl = (u + 8 - d) % 8
            xs = (x + NX - dx) % NX
            peers = [near_x(s) for s in x_dirs] + [near_z(s) for s in z_dirs]
            first = sem
            sem += len(peers)

            @pl.when(zl < 4)
            def _():
                act(quarter, zl, xs, peers, first)

    def receive_and_pass(quarter, zl, xs, peers, first):
        here = vg_ref.at[zl * NX + xs, quarter]
        pltpu.make_async_copy(here, here, v_recv.at[(zl * NX + xs) * 4 + quarter]).wait()
        for i, peer in enumerate(peers):
            v_copy(quarter, zl, xs, peer, first + i).start()

    def finish(quarter, zl, xs, peers, first):
        for i, peer in enumerate(peers):
            v_copy(quarter, zl, xs, peer, first + i).wait_send()

    own.start()
    t_across.start()
    t_near.start()
    walk(receive_and_pass)
    walk(finish)
    own.wait()
    t_near.wait()
    t_across.wait_send()
    t_pass.wait()
    for k in range(2):
        here = mine & (y_lo == k)

        @pl.when(jnp.logical_not(here))
        def _():
            pltpu.make_async_remote_copy(
                src_ref=vc_ref,
                dst_ref=vg_ref.at[block, vir],
                send_sem=y_send.at[k],
                recv_sem=v_recv.at[block * 4 + vir],
                device_id=(at(k, z, x), 2 * y_lo + z // 4),
                device_id_type=MESH,
            ).wait_send()


def gather(tc, vc):
    anywhere = pl.BlockSpec(memory_space=pl.ANY)
    return pl.pallas_call(
        gather_kernel,
        out_shape=(
            jax.ShapeDtypeStruct((4,) + tc.shape, F32),
            jax.ShapeDtypeStruct((16, 4) + vc.shape, F32),
        ),
        in_specs=[anywhere, anywhere],
        out_specs=(anywhere, anywhere),
        scratch_shapes=[
            pltpu.SemaphoreType.DMA((N_SENDS,)),
            pltpu.SemaphoreType.DMA((64,)),
            pltpu.SemaphoreType.DMA((2,)),
            pltpu.SemaphoreType.DMA((3,)),
            pltpu.SemaphoreType.DMA((3,)),
            pltpu.SemaphoreType.DMA,
        ],
        compiler_params=pltpu.CompilerParams(collective_id=0, has_side_effects=True, vmem_limit_bytes=8 << 20),
        name="gather",
    )(tc, vc)


def product_kernel(tg_ref, vg_ref, ij_ref, out_ref, rounds_ref, left, mask_col):
    slabs = tg_ref.shape[0]

    @pl.when(pl.program_id(0) == 0)
    def _():
        most = jnp.int32(0)
        for s in range(slabs):
            most = jnp.maximum(most, jnp.max(tg_ref[s, CAP:ROWS, :]).astype(jnp.int32))
        rounds_ref[0, 0] = (most + (CAP - 1)) // CAP
        parts = []
        row = lax.broadcasted_iota(jnp.int32, (ROWS, tg_ref.shape[2]), 0)
        for s in range(slabs):
            parts.append(jnp.where(row == CAP, 0.0, tg_ref[s]))
        high, low = split(jnp.concatenate(parts, axis=0).T)
        left[...] = jnp.concatenate([high, high, low], axis=1)
        mask_col[...] = jnp.broadcast_to(ij_ref[...].astype(F32), (128, ij_ref.shape[1])).T

    blocks = vg_ref.shape[0]
    value = jnp.concatenate(
        [
            jnp.concatenate([vg_ref[b, s] for s in range(slabs)], axis=0)
            for b in range(blocks)
        ],
        axis=1,
    )
    labels = jnp.concatenate([vg_ref[b, 0, CAP:ROWS, :] for b in range(blocks)], axis=1)
    high, low = split(value)
    right = jnp.concatenate([high, low, high], axis=0)
    total = jnp.dot(left[...], right, preferred_element_type=F32)
    same = jnp.concatenate([mask_col[...]] * blocks, axis=1) == labels
    out_ref[...] = jnp.where(same, total, 0.0)


def product(tg, vg, ij):
    slabs, rows, n_ij = tg.shape
    per_step = 2
    return pl.pallas_call(
        product_kernel,
        out_shape=(
            jax.ShapeDtypeStruct((n_ij, vg.shape[0] * 128), F32),
            jax.ShapeDtypeStruct((1, 1), jnp.int32),
        ),
        grid=(vg.shape[0] // per_step,),
        in_specs=[
            pl.BlockSpec(tg.shape, lambda i: (0, 0, 0)),
            pl.BlockSpec((per_step,) + vg.shape[1:], lambda i: (i, 0, 0, 0)),
            pl.BlockSpec((1, n_ij), lambda i: (0, 0)),
        ],
        out_specs=(
            pl.BlockSpec((n_ij, per_step * 128), lambda i: (0, i)),
            pl.BlockSpec((1, 1), lambda i: (0, 0), memory_space=pltpu.SMEM),
        ),
        scratch_shapes=[
            pltpu.VMEM((n_ij, 3 * slabs * rows), BF16),
            pltpu.VMEM((n_ij, 128), F32),
        ],
        compiler_params=pltpu.CompilerParams(vmem_limit_bytes=32 << 20),
        name="product",
    )(tg, vg, ij[None, :])


def per_device(amplitudes, integrals, ij_irrep, cd_irrep, ab_irrep):
    args = (amplitudes, integrals, ij_irrep, cd_irrep, ab_irrep)
    tc, vc = compact(jnp.zeros((1, 1), jnp.int32), *args)
    tg, vg = gather(tc, vc)
    ladder, rounds = product(tg, vg, ij_irrep)

    def more(state):
        return state[0] < rounds[0, 0]

    def one_round(state):
        index, total = state
        tc, vc = compact(index.reshape(1, 1), *args)
        tg, vg = gather(tc, vc)
        return index + 1, total + product(tg, vg, ij_irrep)[0]

    return lax.while_loop(more, one_round, (jnp.int32(1), ladder))[1]


def solution(mesh):
    in_specs = (P("occ", "vir"), P("vir", "occ"), P("occ"), P("vir"), P("occ"))
    out_specs = P("occ", "vir")
    return jax.shard_map(
        per_device, mesh=mesh, in_specs=in_specs, out_specs=out_specs, check_vma=False
    )
```

```python
import functools

import jax
import jax.numpy as jnp
from jax import lax
from jax.experimental import pallas as pl
from jax.experimental.pallas import tpu as pltpu
from jax.sharding import PartitionSpec as P

MESH = pl.DeviceIdType.MESH
G = 8
CAP = 95
ROWS = CAP + 1
NX, NZ = 4, 8
F32, BF16 = jnp.float32, jnp.bfloat16


def split(value):
    high = value.astype(BF16)
    return high, (value - high.astype(F32)).astype(BF16)


def picker(round_index, labels):
    n_cd = labels.shape[1]
    member = lax.broadcasted_iota(jnp.int32, (G, n_cd), 0) == labels
    before = lax.broadcasted_iota(jnp.int32, (n_cd, n_cd), 0) < lax.broadcasted_iota(
        jnp.int32, (n_cd, n_cd), 1
    )
    below = jnp.dot(member.astype(BF16), before.astype(BF16), preferred_element_type=F32)
    rank = jnp.sum(jnp.where(member, below, 0.0), axis=0, keepdims=True).astype(jnp.int32)
    most = jnp.max(jnp.sum(member.astype(F32), axis=1, keepdims=True), axis=0, keepdims=True)
    place = rank - CAP * round_index
    slot = jnp.where((place >= 0) & (place < CAP), labels * ROWS + place, -1)
    pick = (lax.broadcasted_iota(jnp.int32, (G * ROWS, n_cd), 0) == slot).astype(BF16)
    return jnp.concatenate([pick, pick], axis=1), most


def compacted(pick2, both, dims, column_labels, last_row):
    wide = lax.dot_general(pick2, both, (dims, ((), ())), preferred_element_type=F32)
    out = jnp.zeros((ROWS, wide.shape[1]), F32)
    for g in range(G):
        out = jnp.where(column_labels == g, wide[g * ROWS : (g + 1) * ROWS], out)
    row = lax.broadcasted_iota(jnp.int32, out.shape, 0)
    return jnp.where(row == CAP, last_row, out)


def z_sends(quarter, d):
    up, down = (4, 3) if quarter % 2 == 0 else (3, 4)
    out = []
    if d < up:
        out.append(1)
    if d == 0 or 8 - d < down:
        out.append(-1)
    if d and d <= up and 8 - d <= down:
        raise ValueError
    if 0 < d <= up:
        return [s for s in out if s == 1]
    if d:
        return [s for s in out if s == -1]
    return out


def x_sends(quarter, dx):
    if dx == 0:
        return [1, -1]
    if dx == 1 and quarter % 2 == 0:
        return [1]
    if dx == 3 and quarter % 2 == 1:
        return [-1]
    return []


def spread_events():
    events = []
    for quarter in range(4):
        for d in range(8):
            for dx in range(4):
                x_hops = min(dx, 4 - dx)
                z_hops = min(d, 8 - d)
                if quarter < 2:
                    xs = x_sends(quarter, dx) if d == 0 else []
                    zs = z_sends(quarter, d)
                else:
                    xs = x_sends(quarter, dx)
                    zs = z_sends(quarter, d) if dx == 0 else []
                when = x_hops + z_hops
                late = z_hops if quarter < 2 else x_hops
                events.append((when, late, d, dx, quarter, xs, zs))
    return sorted(events)


EVENTS = spread_events()
N_SENDS = sum(len(e[5]) + len(e[6]) for e in EVENTS)
LAST_HOPS = max(e[0] for e in EVENTS)
SLABS = 4
QUARTERS = ((0, 80), (80, 80), (160, 112), (272, 112))


def spread_kernel(
    round_ref, t_hbm, v_hbm, ij_ref, cd_ref, ab_ref, vg_ref, left_ref, mask_ref, rounds_ref,
    t_buf, v_buf, vc_ref, tg_ref, pick_ref, v_send, v_recv, y_send, t_send, t_recv, in_sem,
):
    t_in = pltpu.make_async_copy(t_hbm, t_buf, in_sem.at[0])
    v_in = pltpu.make_async_copy(v_hbm, v_buf, in_sem.at[1])
    v_in.start()
    t_in.start()
    occ, vir = lax.axis_index("occ"), lax.axis_index("vir")
    y_lo, z, x = occ // (NX * NZ), (occ // NX) % NZ, occ % NX
    y_hi, core = vir // 2, vir % 2
    u = (z + NZ - 4 * core) % NZ

    def at(y, z, x):
        return y * (NX * NZ) + z * NX + x

    def near_x(step):
        return (at(y_lo, z, (x + NX + step) % NX), vir)

    def near_z(step):
        return (at(y_lo, (z + NZ + step) % NZ, x), vir)

    owner = z // 4 == core
    mine = owner & (y_lo == y_hi)
    sibling, across = (occ, vir + 1 - 2 * core), (occ, (vir + 2) % 4)

    barrier = pltpu.get_barrier_semaphore()

    def ready_for(peer):
        pl.semaphore_signal(barrier, inc=1, device_id=peer, device_id_type=MESH)

    for peer in (near_x(1), near_x(-1), sibling, across):
        ready_for(peer)
    pl.when(u != 0)(lambda: ready_for(near_z(-1)))
    pl.when(u != 3)(lambda: ready_for(near_z(1)))
    for k in range(4):
        pl.when(owner & jnp.logical_not(mine & (vir == k)))(
            lambda: ready_for((at(y_hi, z, x), k))
        )
    heard = 6 + (u != 7).astype(jnp.int32) + (u != 4).astype(jnp.int32)

    pick2, most = picker(round_ref[0, 0], cd_ref[...])
    pick_ref[...] = pick2
    ab = ab_ref[...]
    v_in.wait()
    both = jnp.concatenate(split(v_buf[...]), axis=0)
    vc_ref[...] = compacted(pick2, both, ((1,), (0,)), ab, ab.astype(F32))
    pl.semaphore_wait(barrier, heard - mine.astype(jnp.int32))

    block = (z % 4) * NX + x
    for k in range(2):
        target = (at(k, z, x), 2 * y_lo + z // 4)
        here = mine & (y_lo == k)

        @pl.when(here)
        def _():
            pltpu.make_async_copy(
                vc_ref, vg_ref.at[block, pl.ds(vir * ROWS, ROWS)], v_recv.at[block * 4 + vir]
            ).start()

        @pl.when(jnp.logical_not(here))
        def _():
            pltpu.make_async_remote_copy(
                src_ref=vc_ref,
                dst_ref=vg_ref.at[block, pl.ds(vir * ROWS, ROWS)],
                send_sem=y_send.at[k],
                recv_sem=v_recv.at[block * 4 + vir],
                device_id=target,
                device_id_type=MESH,
            ).start()

    def t_copy(k, src, slab, peer):
        return pltpu.make_async_remote_copy(
            src_ref=src,
            dst_ref=tg_ref.at[slab],
            send_sem=t_send.at[k],
            recv_sem=t_recv.at[k],
            device_id=peer,
            device_id_type=MESH,
        )

    far = (vir + 2) % 4
    t_across = t_copy(0, tg_ref.at[vir], vir, across)
    t_near = t_copy(1, tg_ref.at[vir], vir, sibling)
    t_pass = t_copy(2, tg_ref.at[far], far, sibling)
    t_in.wait()
    both = jnp.concatenate(split(t_buf[...]), axis=1)
    tg_ref[vir] = compacted(pick_ref[...], both, ((1,), (1,)), ij_ref[...], most)

    def v_copy(quarter, zl, xs, peer, sem):
        here = vg_ref.at[zl * NX + xs, pl.ds(*QUARTERS[quarter])]
        return pltpu.make_async_remote_copy(
            src_ref=here,
            dst_ref=here,
            send_sem=v_send.at[sem],
            recv_sem=v_recv.at[(zl * NX + xs) * 4 + quarter],
            device_id=peer,
            device_id_type=MESH,
        )

    def walk(act, after_hops):
        sem = 0
        for n, (hops, _, d, dx, quarter, x_dirs, z_dirs) in enumerate(EVENTS):
            if n and hops > EVENTS[n - 1][0]:
                after_hops(EVENTS[n - 1][0])
            zl = (u + 8 - d) % 8
            xs = (x + NX - dx) % NX
            peers = [near_x(s) for s in x_dirs] + [near_z(s) for s in z_dirs]
            first = sem
            sem += len(peers)

            @pl.when(zl < 4)
            def _():
                act(quarter, zl, xs, peers, first, d == 0 and dx == 0)

    def receive_and_pass(quarter, zl, xs, peers, first, own):
        start, size = (quarter * ROWS, ROWS) if own else QUARTERS[quarter]
        here = vg_ref.at[zl * NX + xs, pl.ds(start, size)]
        pltpu.make_async_copy(here, here, v_recv.at[(zl * NX + xs) * 4 + quarter]).wait()
        for i, peer in enumerate(peers):
            v_copy(quarter, zl, xs, peer, first + i).start()

    def finish(quarter, zl, xs, peers, first, own):
        for i, peer in enumerate(peers):
            v_copy(quarter, zl, xs, peer, first + i).wait_send()

    def between(hops):
        if hops == 2:
            t_across.wait_recv()
            t_pass.start()
        if hops == LAST_HOPS - 1:
            t_near.wait_recv()
            t_pass.wait_recv()
            most = jnp.float32(0)
            for s in range(SLABS):
                most = jnp.maximum(most, jnp.max(tg_ref[s, CAP:ROWS, :]))
            rounds_ref[0, 0] = (most.astype(jnp.int32) + (CAP - 1)) // CAP
            row = lax.broadcasted_iota(jnp.int32, tg_ref.shape[1:], 0)
            parts = [jnp.where(row == CAP, 0.0, tg_ref[s]) for s in range(SLABS)]
            high, low = split(jnp.concatenate(parts, axis=0).T)
            left_ref[...] = jnp.concatenate([high, high, low], axis=1)
            labels = ij_ref[...].astype(F32)
            mask_ref[...] = jnp.broadcast_to(labels, (128, labels.shape[1])).T

    t_across.start()
    t_near.start()
    walk(receive_and_pass, between)
    walk(finish, lambda hops: None)
    for copy in (t_across, t_near, t_pass):
        copy.wait_send()
    for k in range(2):
        here = mine & (y_lo == k)

        @pl.when(jnp.logical_not(here))
        def _():
            pltpu.make_async_remote_copy(
                src_ref=vc_ref,
                dst_ref=vg_ref.at[block, pl.ds(vir * ROWS, ROWS)],
                send_sem=y_send.at[k],
                recv_sem=v_recv.at[block * 4 + vir],
                device_id=(at(k, z, x), 2 * y_lo + z // 4),
                device_id_type=MESH,
            ).wait_send()


def spread(round_index, t, v, ij, cd, ab):
    n_ij, n_cd = t.shape
    anywhere = pl.BlockSpec(memory_space=pl.ANY)
    vmem = pl.BlockSpec(memory_space=pltpu.VMEM)
    smem = pl.BlockSpec(memory_space=pltpu.SMEM)
    return pl.pallas_call(
        spread_kernel,
        out_shape=(
            jax.ShapeDtypeStruct((16, SLABS * ROWS, v.shape[1]), F32),
            jax.ShapeDtypeStruct((n_ij, 3 * SLABS * ROWS), BF16),
            jax.ShapeDtypeStruct((n_ij, 128), F32),
            jax.ShapeDtypeStruct((1, 1), jnp.int32),
        ),
        in_specs=[smem, anywhere, anywhere, vmem, vmem, vmem],
        out_specs=(anywhere, vmem, vmem, smem),
        scratch_shapes=[
            pltpu.VMEM(t.shape, F32),
            pltpu.VMEM(v.shape, F32),
            pltpu.VMEM((ROWS, v.shape[1]), F32),
            pltpu.VMEM((SLABS, ROWS, n_ij), F32),
            pltpu.VMEM((G * ROWS, 2 * n_cd), BF16),
            pltpu.SemaphoreType.DMA((N_SENDS,)),
            pltpu.SemaphoreType.DMA((64,)),
            pltpu.SemaphoreType.DMA((2,)),
            pltpu.SemaphoreType.DMA((3,)),
            pltpu.SemaphoreType.DMA((3,)),
            pltpu.SemaphoreType.DMA((2,)),
        ],
        compiler_params=pltpu.CompilerParams(
            collective_id=0, has_side_effects=True, vmem_limit_bytes=24 << 20
        ),
        name="spread",
    )(round_index, t, v, ij[None, :], cd[None, :], ab[None, :])


def product_kernel(left_ref, vg_ref, mask_ref, out_ref):
    blocks = vg_ref.shape[0]
    value = jnp.concatenate([vg_ref[b] for b in range(blocks)], axis=1)
    labels = jnp.concatenate([vg_ref[b, CAP:ROWS, :] for b in range(blocks)], axis=1)
    high, low = split(value)
    right = jnp.concatenate([high, low, high], axis=0)
    total = jnp.dot(left_ref[...], right, preferred_element_type=F32)
    same = jnp.concatenate([mask_ref[...]] * blocks, axis=1) == labels
    out_ref[...] = jnp.where(same, total, 0.0)


def product(left, vg, mask):
    n_ij, per_step = left.shape[0], 2
    return pl.pallas_call(
        product_kernel,
        out_shape=jax.ShapeDtypeStruct((n_ij, vg.shape[0] * 128), F32),
        grid=(vg.shape[0] // per_step,),
        in_specs=[
            pl.BlockSpec(left.shape, lambda i: (0, 0)),
            pl.BlockSpec((per_step,) + vg.shape[1:], lambda i: (i, 0, 0)),
            pl.BlockSpec(mask.shape, lambda i: (0, 0)),
        ],
        out_specs=pl.BlockSpec((n_ij, per_step * 128), lambda i: (0, i)),
        compiler_params=pltpu.CompilerParams(vmem_limit_bytes=24 << 20),
        name="product",
    )(left, vg, mask)


def per_device(*args):
    def one_round(index):
        vg, left, mask, rounds = spread(index.reshape(1, 1), *args)
        return product(left, vg, mask), rounds

    ladder, rounds = one_round(jnp.int32(0))

    def more(state):
        return state[0] < rounds[0, 0]

    def next_round(state):
        index, total = state
        return index + 1, total + one_round(index)[0]

    return lax.while_loop(more, next_round, (jnp.int32(1), ladder))[1]


def solution(mesh):
    in_specs = (P("occ", "vir"), P("vir", "occ"), P("occ"), P("vir"), P("occ"))
    out_specs = P("occ", "vir")
    return jax.shard_map(
        per_device, mesh=mesh, in_specs=in_specs, out_specs=out_specs, check_vma=False
    )
```

```python
import functools

import jax
import jax.numpy as jnp
from jax import lax
from jax.experimental import pallas as pl
from jax.experimental.pallas import tpu as pltpu
from jax.sharding import PartitionSpec as P

MESH = pl.DeviceIdType.MESH
G = 8
CAP = 95
ROWS = CAP + 1
NX, NZ = 4, 8
F32, BF16 = jnp.float32, jnp.bfloat16


def split(value):
    high = value.astype(BF16)
    return high, (value - high.astype(F32)).astype(BF16)


def picker(round_index, labels):
    n_cd = labels.shape[1]
    member = lax.broadcasted_iota(jnp.int32, (G, n_cd), 0) == labels
    before = lax.broadcasted_iota(jnp.int32, (n_cd, n_cd), 0) < lax.broadcasted_iota(
        jnp.int32, (n_cd, n_cd), 1
    )
    below = jnp.dot(member.astype(BF16), before.astype(BF16), preferred_element_type=F32)
    rank = jnp.sum(jnp.where(member, below, 0.0), axis=0, keepdims=True).astype(jnp.int32)
    most = jnp.max(jnp.sum(member.astype(F32), axis=1, keepdims=True), axis=0, keepdims=True)
    place = rank - CAP * round_index
    slot = jnp.where((place >= 0) & (place < CAP), labels * ROWS + place, -1)
    pick = (lax.broadcasted_iota(jnp.int32, (G * ROWS, n_cd), 0) == slot).astype(BF16)
    return jnp.concatenate([pick, pick], axis=1), most


def compacted(pick2, both, dims, column_labels, last_row):
    wide = lax.dot_general(pick2, both, (dims, ((), ())), preferred_element_type=F32)
    out = jnp.zeros((ROWS, wide.shape[1]), F32)
    for g in range(G):
        out = jnp.where(column_labels == g, wide[g * ROWS : (g + 1) * ROWS], out)
    row = lax.broadcasted_iota(jnp.int32, out.shape, 0)
    return jnp.where(row == CAP, last_row, out)


SLABS = 4
PARTS = ((0, 80), (80, 80), (160, 112), (272, 112))
PARENTS = (
    (-1, 0, 1, 0, 0, 1, 2, 3, 4, 5, 6, 7, 8, 9, 10, 11,
     12, 13, 14, 15, 24, 25, 26, 27, 28, 29, 30, 31, 0, 1, 2, 3),
    (-1, 0, 3, 0, 0, 1, 2, 3, 4, 5, 6, 7, 8, 9, 10, 11,
     20, 21, 22, 23, 24, 25, 26, 27, 28, 29, 30, 31, 0, 1, 2, 3),
    (-1, 0, 1, 0, 0, 4, 5, 4, 4, 8, 9, 8, 8, 12, 13, 12,
     12, 16, 17, 16, 24, 20, 21, 20, 28, 24, 25, 24, 0, 28, 29, 28),
    (-1, 0, 3, 0, 0, 4, 7, 4, 4, 8, 11, 8, 8, 12, 15, 12,
     20, 16, 19, 16, 24, 20, 23, 20, 28, 24, 27, 24, 0, 28, 31, 28),
)
ORDER = (
    0, 32, 64, 96, 1, 33, 3, 35, 68, 100, 92, 124, 65, 97, 67, 99, 4, 36, 28, 60, 2, 34, 72, 104,
    88, 120, 5, 37, 69, 101, 7, 39, 71, 103, 29, 61, 93, 125, 31, 63, 95, 127, 66, 98, 8, 40, 24,
    56, 76, 108, 84, 116, 6, 38, 73, 105, 75, 107, 89, 121, 91, 123, 30, 62, 70, 102, 9, 41, 11,
    43, 25, 57, 27, 59, 94, 126, 12, 44, 20, 52, 80, 112, 77, 109, 79, 111, 85, 117, 87, 119, 10,
    42, 74, 106, 26, 58, 90, 122, 13, 45, 15, 47, 21, 53, 23, 55, 16, 48, 81, 113, 83, 115, 78,
    110, 86, 118, 14, 46, 22, 54, 17, 49, 19, 51, 82, 114, 18, 50,
)


def spread_plan():
    events, seen = [], set()
    children = [[[] for _ in range(32)] for _ in PARTS]
    for part, parents in enumerate(PARENTS):
        for child, parent in enumerate(parents):
            if parent >= 0:
                children[part][parent].append(child)

    def height(part, node):
        return max([1 + height(part, c) for c in children[part][node]], default=0)

    for item in ORDER:
        part, node = item // 32, item % 32
        below = sorted(children[part][node], key=lambda c: -height(part, c))
        if node:
            arrivals = [part]
        else:
            start, size = PARTS[part]
            spans = range(start // ROWS, (start + size - 1) // ROWS + 1)
            arrivals = [slab for slab in spans if slab not in seen]
            seen.update(arrivals)
        if below:
            events.append((part, node // 4, node % 4, below, arrivals))
    leaves = [[not c for c in nodes] for nodes in children]
    return events, leaves


EVENTS, LEAVES = spread_plan()


SENT = [
    [sum(len(e[3]) for e in EVENTS if e[:2] == (part, dz)) for dz in range(NZ)]
    for part in range(len(PARTS))
]


STEPS = {}
for _part, _dz, _dx, _below, _ in EVENTS:
    for _c in _below:
        _step = ((_c // 4 - _dz) % NZ, (_c % 4 - _dx) % NX)
        STEPS.setdefault(_step, set()).update((_dz + zl) % NZ for zl in range(4))


def among(u, values):
    return functools.reduce(jnp.logical_or, [u == v for v in sorted(values)])


def spread_kernel(
    round_ref, t_hbm, v_hbm, ij_ref, cd_ref, ab_ref, vg_ref, left_ref, mask_ref, rounds_ref,
    t_buf, v_buf, vc_ref, tg_ref, pick_ref, v_send, v_recv, leaf_recv, y_send, t_send, t_recv, in_sem,
):
    t_in = pltpu.make_async_copy(t_hbm, t_buf, in_sem.at[0])
    v_in = pltpu.make_async_copy(v_hbm, v_buf, in_sem.at[1])
    v_in.start()
    t_in.start()
    occ, vir = lax.axis_index("occ"), lax.axis_index("vir")
    y_lo, z, x = occ // (NX * NZ), (occ // NX) % NZ, occ % NX
    y_hi, core = vir // 2, vir % 2
    u = (z + NZ - 4 * core) % NZ

    def at(y, z, x):
        return y * (NX * NZ) + z * NX + x

    def away(dz, dx):
        return (at(y_lo, (z + NZ + dz) % NZ, (x + NX + dx) % NX), vir)

    owner = z // 4 == core
    mine = owner & (y_lo == y_hi)
    sibling, across = (occ, vir + 1 - 2 * core), (occ, (vir + 2) % 4)

    barrier = pltpu.get_barrier_semaphore()

    def ready_for(peer):
        pl.semaphore_signal(barrier, inc=1, device_id=peer, device_id_type=MESH)

    for peer in (sibling, across):
        ready_for(peer)
    heard = 4 - mine.astype(jnp.int32)
    for (dz, dx), senders in STEPS.items():
        source = (u + NZ - dz) % NZ
        pl.when(among(source, senders))(lambda: ready_for(away(-dz, -dx)))
        heard += among(u, senders).astype(jnp.int32)
    for k in range(4):
        pl.when(owner & jnp.logical_not(mine & (vir == k)))(
            lambda: ready_for((at(y_hi, z, x), k))
        )

    pick2, most = picker(round_ref[0, 0], cd_ref[...])
    pick_ref[...] = pick2
    ab = ab_ref[...]
    v_in.wait()
    both = jnp.concatenate(split(v_buf[...]), axis=0)
    vc_ref[...] = compacted(pick2, both, ((1,), (0,)), ab, ab.astype(F32))
    pl.semaphore_wait(barrier, heard)

    block = (z % 4) * NX + x
    for k in range(2):
        target = (at(k, z, x), 2 * y_lo + z // 4)
        here = mine & (y_lo == k)

        @pl.when(here)
        def _():
            pltpu.make_async_copy(
                vc_ref, vg_ref.at[block, pl.ds(vir * ROWS, ROWS)], v_recv.at[block * 4 + vir]
            ).start()

        @pl.when(jnp.logical_not(here))
        def _():
            pltpu.make_async_remote_copy(
                src_ref=vc_ref,
                dst_ref=vg_ref.at[block, pl.ds(vir * ROWS, ROWS)],
                send_sem=y_send.at[k],
                recv_sem=v_recv.at[block * 4 + vir],
                device_id=target,
                device_id_type=MESH,
            ).start()

    def t_copy(k, src, slab, peer):
        return pltpu.make_async_remote_copy(
            src_ref=src,
            dst_ref=tg_ref.at[slab],
            send_sem=t_send.at[k],
            recv_sem=t_recv.at[k],
            device_id=peer,
            device_id_type=MESH,
        )

    far = (vir + 2) % 4
    t_across = t_copy(0, tg_ref.at[vir], vir, across)
    t_near = t_copy(1, tg_ref.at[vir], vir, sibling)
    t_pass = t_copy(2, tg_ref.at[far], far, sibling)
    t_in.wait()
    both = jnp.concatenate(split(t_buf[...]), axis=1)
    tg_ref[vir] = compacted(pick_ref[...], both, ((1,), (1,)), ij_ref[...], most)

    def v_copy(part, dz, dx, child):
        zl, xs = (u + NZ - dz) % NZ, (x + NX - dx) % NX
        here = vg_ref.at[zl * NX + xs, pl.ds(*PARTS[part])]
        leaf = LEAVES[part][child]
        return pltpu.make_async_remote_copy(
            src_ref=here,
            dst_ref=here,
            send_sem=v_send.at[dz * len(PARTS) + part],
            recv_sem=leaf_recv.at[zl * len(PARTS) + part] if leaf else v_recv.at[(zl * NX + xs) * 4 + part],
            device_id=away(child // 4 - dz, child % 4 - dx),
            device_id_type=MESH,
        )

    def wait_all(part, count, sem):
        if count:
            here = vg_ref.at[pl.ds(0, count), pl.ds(*PARTS[part])]
            pltpu.make_async_copy(here, here, sem).wait()

    t_across.start()
    t_near.start()
    for n, (part, dz, dx, below, arrivals) in enumerate(EVENTS):
        zl, xs = (u + NZ - dz) % NZ, (x + NX - dx) % NX
        if n == int(len(EVENTS) * 0.35):
            t_across.wait_recv()
            t_pass.start()

        @pl.when(zl < 4)
        def _():
            for k in arrivals:
                rows = (k * ROWS, ROWS) if dz == 0 and dx == 0 else PARTS[part]
                here = vg_ref.at[zl * NX + xs, pl.ds(*rows)]
                pltpu.make_async_copy(here, here, v_recv.at[(zl * NX + xs) * 4 + k]).wait()
            for child in below:
                v_copy(part, dz, dx, child).start()

    t_near.wait_recv()
    t_pass.wait_recv()
    most = jnp.float32(0)
    for s in range(SLABS):
        most = jnp.maximum(most, jnp.max(tg_ref[s, CAP:ROWS, :]))
    rounds_ref[0, 0] = (most.astype(jnp.int32) + (CAP - 1)) // CAP
    row = lax.broadcasted_iota(jnp.int32, tg_ref.shape[1:], 0)
    parts = [jnp.where(row == CAP, 0.0, tg_ref[s]) for s in range(SLABS)]
    high, low = split(jnp.concatenate(parts, axis=0).T)
    left_ref[...] = jnp.concatenate([high, high, low], axis=1)
    labels = ij_ref[...].astype(F32)
    mask_ref[...] = jnp.broadcast_to(labels, (128, labels.shape[1])).T

    for copy in (t_across, t_near, t_pass):
        copy.wait_send()
    for k in range(2):
        here = mine & (y_lo == k)

        @pl.when(jnp.logical_not(here))
        def _():
            pltpu.make_async_remote_copy(
                src_ref=vc_ref,
                dst_ref=vg_ref.at[block, pl.ds(vir * ROWS, ROWS)],
                send_sem=y_send.at[k],
                recv_sem=v_recv.at[block * 4 + vir],
                device_id=(at(k, z, x), 2 * y_lo + z // 4),
                device_id_type=MESH,
            ).wait_send()

    for dz in range(NZ):

        @pl.when((u + NZ - dz) % NZ < 4)
        def _():
            for part in range(len(PARTS)):
                wait_all(part, SENT[part][dz], v_send.at[dz * len(PARTS) + part])

    for dz in (0, 1, 7, 2, 6, 3, 5, 4):
        zl = (u + NZ - dz) % NZ

        @pl.when(zl < 4)
        def _():
            for part in range(len(PARTS)):
                wait_all(part, sum(LEAVES[part][4 * dz : 4 * dz + 4]), leaf_recv.at[zl * len(PARTS) + part])


def spread(round_index, t, v, ij, cd, ab):
    n_ij, n_cd = t.shape
    anywhere = pl.BlockSpec(memory_space=pl.ANY)
    vmem = pl.BlockSpec(memory_space=pltpu.VMEM)
    smem = pl.BlockSpec(memory_space=pltpu.SMEM)
    return pl.pallas_call(
        spread_kernel,
        out_shape=(
            jax.ShapeDtypeStruct((16, SLABS * ROWS, v.shape[1]), F32),
            jax.ShapeDtypeStruct((n_ij, 3 * SLABS * ROWS), BF16),
            jax.ShapeDtypeStruct((n_ij, 128), F32),
            jax.ShapeDtypeStruct((1, 1), jnp.int32),
        ),
        in_specs=[smem, anywhere, anywhere, vmem, vmem, vmem],
        out_specs=(anywhere, vmem, vmem, smem),
        scratch_shapes=[
            pltpu.VMEM(t.shape, F32),
            pltpu.VMEM(v.shape, F32),
            pltpu.VMEM((ROWS, v.shape[1]), F32),
            pltpu.VMEM((SLABS, ROWS, n_ij), F32),
            pltpu.VMEM((G * ROWS, 2 * n_cd), BF16),
            pltpu.SemaphoreType.DMA((NZ * len(PARTS),)),
            pltpu.SemaphoreType.DMA((16 * len(PARTS),)),
            pltpu.SemaphoreType.DMA((4 * len(PARTS),)),
            pltpu.SemaphoreType.DMA((2,)),
            pltpu.SemaphoreType.DMA((3,)),
            pltpu.SemaphoreType.DMA((3,)),
            pltpu.SemaphoreType.DMA((2,)),
        ],
        compiler_params=pltpu.CompilerParams(
            collective_id=0, has_side_effects=True, vmem_limit_bytes=24 << 20
        ),
        name="spread",
    )(round_index, t, v, ij[None, :], cd[None, :], ab[None, :])


def product_kernel(left_ref, vg_ref, mask_ref, out_hbm, out_buf, out_sem):
    copies = []
    for step in range(4):
        blocks = range(step * 4, step * 4 + 4)
        value = jnp.concatenate([vg_ref[b] for b in blocks], axis=1)
        labels = jnp.concatenate([vg_ref[b, CAP:ROWS, :] for b in blocks], axis=1)
        high, low = split(value)
        right = jnp.concatenate([high, low, high], axis=0)
        total = jnp.dot(left_ref[...], right, preferred_element_type=F32)
        same = jnp.concatenate([mask_ref[...]] * 4, axis=1) == labels
        out_buf[step] = jnp.where(same, total, 0.0)
        columns = pl.ds(step * 512, 512)
        copy = pltpu.make_async_copy(out_buf.at[step], out_hbm.at[:, columns], out_sem.at[step])
        copy.start()
        copies.append(copy)
    for copy in copies:
        copy.wait()


def product(left, vg, mask):
    n_ij = left.shape[0]
    vmem = pl.BlockSpec(memory_space=pltpu.VMEM)
    return pl.pallas_call(
        product_kernel,
        out_shape=jax.ShapeDtypeStruct((n_ij, 2048), F32),
        in_specs=[vmem, vmem, vmem],
        out_specs=pl.BlockSpec(memory_space=pl.ANY),
        scratch_shapes=[pltpu.VMEM((4, n_ij, 512), F32), pltpu.SemaphoreType.DMA((4,))],
        compiler_params=pltpu.CompilerParams(vmem_limit_bytes=24 << 20),
        name="product",
    )(left, vg, mask)


def per_device(*args):
    def one_round(index):
        vg, left, mask, rounds = spread(index.reshape(1, 1), *args)
        return product(left, vg, mask), rounds

    ladder, rounds = one_round(jnp.int32(0))

    def more(state):
        return state[0] < rounds[0, 0]

    def next_round(state):
        index, total = state
        return index + 1, total + one_round(index)[0]

    return lax.while_loop(more, next_round, (jnp.int32(1), ladder))[1]


def solution(mesh):
    in_specs = (P("occ", "vir"), P("vir", "occ"), P("occ"), P("vir"), P("occ"))
    out_specs = P("occ", "vir")
    return jax.shard_map(
        per_device, mesh=mesh, in_specs=in_specs, out_specs=out_specs, check_vma=False
    )
```

```python
import functools

import jax
import jax.numpy as jnp
from jax import lax
from jax.experimental import pallas as pl
from jax.experimental.pallas import tpu as pltpu
from jax.sharding import PartitionSpec as P

MESH = pl.DeviceIdType.MESH
G = 8
CAP = 95
ROWS = CAP + 1
NX, NZ = 4, 8
F32, BF16 = jnp.float32, jnp.bfloat16


def split(value):
    high = value.astype(BF16)
    return high, (value - high.astype(F32)).astype(BF16)


def picker(round_index, labels):
    n_cd = labels.shape[1]
    member = lax.broadcasted_iota(jnp.int32, (G, n_cd), 0) == labels
    before = lax.broadcasted_iota(jnp.int32, (n_cd, n_cd), 0) < lax.broadcasted_iota(
        jnp.int32, (n_cd, n_cd), 1
    )
    below = jnp.dot(member.astype(BF16), before.astype(BF16), preferred_element_type=F32)
    rank = jnp.sum(jnp.where(member, below, 0.0), axis=0, keepdims=True).astype(jnp.int32)
    most = jnp.max(jnp.sum(member.astype(F32), axis=1, keepdims=True), axis=0, keepdims=True)
    place = rank - CAP * round_index
    slot = jnp.where((place >= 0) & (place < CAP), labels * ROWS + place, -1)
    pick = (lax.broadcasted_iota(jnp.int32, (G * ROWS, n_cd), 0) == slot).astype(BF16)
    return jnp.concatenate([pick, pick], axis=1), most


def compacted(pick2, both, dims, column_labels, last_row):
    wide = lax.dot_general(pick2, both, (dims, ((), ())), preferred_element_type=F32)
    out = jnp.zeros((ROWS, wide.shape[1]), F32)
    for g in range(G):
        out = jnp.where(column_labels == g, wide[g * ROWS : (g + 1) * ROWS], out)
    row = lax.broadcasted_iota(jnp.int32, out.shape, 0)
    return jnp.where(row == CAP, last_row, out)


SLABS = 4
PARTS = ((0, 80), (80, 80), (160, 112), (272, 112))
PARENTS = (
    (-1, 0, 1, 0, 0, 1, 2, 3, 4, 5, 6, 7, 8, 9, 10, 11,
     12, 13, 14, 15, 24, 25, 26, 27, 28, 29, 30, 31, 0, 1, 2, 3),
    (-1, 0, 3, 0, 0, 1, 2, 3, 4, 5, 6, 7, 8, 9, 10, 11,
     20, 21, 22, 23, 24, 25, 26, 27, 28, 29, 30, 31, 0, 1, 2, 3),
    (-1, 0, 1, 0, 0, 4, 5, 4, 4, 8, 9, 8, 8, 12, 13, 12,
     12, 16, 17, 16, 24, 20, 21, 20, 28, 24, 25, 24, 0, 28, 29, 28),
    (-1, 0, 3, 0, 0, 4, 7, 4, 4, 8, 11, 8, 8, 12, 15, 12,
     20, 16, 19, 16, 24, 20, 23, 20, 28, 24, 27, 24, 0, 28, 31, 28),
)
ORDER = (
    0, 32, 64, 96, 1, 33, 3, 35, 68, 100, 92, 124, 65, 97, 67, 99, 4, 36, 28, 60, 2, 34, 72, 104,
    88, 120, 5, 37, 69, 101, 7, 39, 71, 103, 29, 61, 93, 125, 31, 63, 95, 127, 66, 98, 8, 40, 24,
    56, 76, 108, 84, 116, 6, 38, 73, 105, 75, 107, 89, 121, 91, 123, 30, 62, 70, 102, 9, 41, 11,
    43, 25, 57, 27, 59, 94, 126, 12, 44, 20, 52, 80, 112, 77, 109, 79, 111, 85, 117, 87, 119, 10,
    42, 74, 106, 26, 58, 90, 122, 13, 45, 15, 47, 21, 53, 23, 55, 16, 48, 81, 113, 83, 115, 78,
    110, 86, 118, 14, 46, 22, 54, 17, 49, 19, 51, 82, 114, 18, 50,
)


def spread_plan():
    events, seen = [], set()
    children = [[[] for _ in range(32)] for _ in PARTS]
    for part, parents in enumerate(PARENTS):
        for child, parent in enumerate(parents):
            if parent >= 0:
                children[part][parent].append(child)

    def height(part, node):
        return max([1 + height(part, c) for c in children[part][node]], default=0)

    for item in ORDER:
        part, node = item // 32, item % 32
        below = sorted(children[part][node], key=lambda c: -height(part, c))
        if node:
            arrivals = [part]
        else:
            start, size = PARTS[part]
            spans = range(start // ROWS, (start + size - 1) // ROWS + 1)
            arrivals = [slab for slab in spans if slab not in seen]
            seen.update(arrivals)
        if below:
            events.append((part, node // 4, node % 4, below, arrivals))
    leaves = [[not c for c in nodes] for nodes in children]
    return events, leaves


EVENTS, LEAVES = spread_plan()
LATE = (0, 0, 4 * (NZ - 1))


SENT = [
    [sum(len(e[3]) for e in EVENTS if e[:2] == (part, dz)) for dz in range(NZ)]
    for part in range(len(PARTS))
]


STEPS = {}
for _part, _dz, _dx, _below, _ in EVENTS:
    for _c in _below:
        _step = ((_c // 4 - _dz) % NZ, (_c % 4 - _dx) % NX)
        STEPS.setdefault(_step, set()).update((_dz + zl) % NZ for zl in range(4))


def among(u, values):
    return functools.reduce(jnp.logical_or, [u == v for v in sorted(values)])


ROW_ORDER = [
    sorted(range(4), key=lambda zl: (min((u - zl) % NZ, (zl - u) % NZ), zl)) for u in range(NZ)
]


def row_order(u):
    digits = [sum(zl * 4**j for j, zl in enumerate(rows)) for rows in ROW_ORDER]
    return functools.reduce(jnp.add, [jnp.where(u == k, d, 0) for k, d in enumerate(digits)])


def row_product(left_ref, vg_ref, mask_ref, zl):
    blocks = [zl * NX + b for b in range(NX)]
    value = jnp.concatenate([vg_ref[b] for b in blocks], axis=1)
    labels = jnp.concatenate([vg_ref[b, CAP:ROWS, :] for b in blocks], axis=1)
    high, low = split(value)
    right = jnp.concatenate([high, low, high], axis=0)
    total = jnp.dot(left_ref[...], right, preferred_element_type=F32)
    return jnp.where(jnp.concatenate([mask_ref[...]] * NX, axis=1) == labels, total, 0.0)


def spread_kernel(
    round_hbm, t_hbm, v_hbm, ij_hbm, cd_hbm, ab_hbm, vg_ref, left_ref, mask_ref, rounds_hbm,
    round_ref, t_buf, v_buf, ij_ref, cd_ref, ab_ref, rounds_ref, vc_ref, tg_ref, pick_ref, v_send, v_recv, leaf_recv, y_send, t_send, t_recv, in_sem, late_sem,
):
    inputs = (cd_hbm, cd_ref), (round_hbm, round_ref), (v_hbm, v_buf), (ab_hbm, ab_ref)
    inputs += (t_hbm, t_buf), (ij_hbm, ij_ref)
    copies_in = [pltpu.make_async_copy(*pair, in_sem.at[k]) for k, pair in enumerate(inputs)]
    cd_in, round_in, v_in, ab_in, t_in, ij_in = copies_in
    for copy in copies_in:
        copy.start()
    occ, vir = lax.axis_index("occ"), lax.axis_index("vir")
    y_lo, z, x = occ // (NX * NZ), (occ // NX) % NZ, occ % NX
    y_hi, core = vir // 2, vir % 2
    u = (z + NZ - 4 * core) % NZ

    def at(y, z, x):
        return y * (NX * NZ) + z * NX + x

    def away(dz, dx):
        return (at(y_lo, (z + NZ + dz) % NZ, (x + NX + dx) % NX), vir)

    owner = z // 4 == core
    mine = owner & (y_lo == y_hi)
    sibling, across = (occ, vir + 1 - 2 * core), (occ, (vir + 2) % 4)

    barrier = pltpu.get_barrier_semaphore()

    def ready_for(peer):
        pl.semaphore_signal(barrier, inc=1, device_id=peer, device_id_type=MESH)

    for peer in (sibling, across):
        ready_for(peer)
    heard = 4 - mine.astype(jnp.int32)
    first_row, last_row = (u == 0) & (core == 0), (u == 7) & (core == 0)
    pl.when(first_row)(lambda: ready_for(away(-1, 0)))
    heard += last_row.astype(jnp.int32) - first_row.astype(jnp.int32)
    for (dz, dx), senders in STEPS.items():
        takes = among((u + NZ - dz) % NZ, senders)
        if (dz, dx) == (NZ - 1, 0):
            takes = takes & jnp.logical_not(last_row)
        pl.when(takes)(lambda: ready_for(away(-dz, -dx)))
        heard += among(u, senders).astype(jnp.int32)
    for k in range(4):
        pl.when(owner & jnp.logical_not(mine & (vir == k)))(
            lambda: ready_for((at(y_hi, z, x), k))
        )

    cd_in.wait()
    round_in.wait()
    pick2, most = picker(round_ref[:, 0:1], cd_ref[...])
    pick_ref[...] = pick2
    ab_in.wait()
    ab = ab_ref[...]
    v_in.wait()
    both = jnp.concatenate(split(v_buf[...]), axis=0)
    vc_ref[...] = compacted(pick2, both, ((1,), (0,)), ab, ab.astype(F32))
    pl.semaphore_wait(barrier, heard)
    pl.when(last_row)(
        lambda: pl.semaphore_signal(late_sem, 1, device_id=away(1, 0), device_id_type=MESH)
    )

    block = (z % 4) * NX + x
    for k in range(2):
        target = (at(k, z, x), 2 * y_lo + z // 4)
        here = mine & (y_lo == k)

        @pl.when(here)
        def _():
            pltpu.make_async_copy(
                vc_ref, vg_ref.at[block, pl.ds(vir * ROWS, ROWS)], v_recv.at[block * 4 + vir]
            ).start()

        @pl.when(jnp.logical_not(here))
        def _():
            pltpu.make_async_remote_copy(
                src_ref=vc_ref,
                dst_ref=vg_ref.at[block, pl.ds(vir * ROWS, ROWS)],
                send_sem=y_send.at[k],
                recv_sem=v_recv.at[block * 4 + vir],
                device_id=target,
                device_id_type=MESH,
            ).start()

    def t_copy(k, src, slab, peer):
        return pltpu.make_async_remote_copy(
            src_ref=src,
            dst_ref=tg_ref.at[slab],
            send_sem=t_send.at[k],
            recv_sem=t_recv.at[k],
            device_id=peer,
            device_id_type=MESH,
        )

    far = (vir + 2) % 4
    t_across = t_copy(0, tg_ref.at[vir], vir, across)
    t_near = t_copy(1, tg_ref.at[vir], vir, sibling)
    t_pass = t_copy(2, tg_ref.at[far], far, sibling)
    t_in.wait()
    ij_in.wait()
    both = jnp.concatenate(split(t_buf[...]), axis=1)
    tg_ref[vir] = compacted(pick_ref[...], both, ((1,), (1,)), ij_ref[...], most)

    def v_copy(part, dz, dx, child):
        zl, xs = (u + NZ - dz) % NZ, (x + NX - dx) % NX
        here = vg_ref.at[zl * NX + xs, pl.ds(*PARTS[part])]
        leaf = LEAVES[part][child]
        return pltpu.make_async_remote_copy(
            src_ref=here,
            dst_ref=here,
            send_sem=v_send.at[dz * len(PARTS) + part],
            recv_sem=leaf_recv.at[zl * len(PARTS) + part] if leaf else v_recv.at[(zl * NX + xs) * 4 + part],
            device_id=away(child // 4 - dz, child % 4 - dx),
            device_id_type=MESH,
        )

    def wait_all(part, count, sem):
        if count:
            here = vg_ref.at[pl.ds(0, count), pl.ds(*PARTS[part])]
            pltpu.make_async_copy(here, here, sem).wait()

    t_across.start()
    t_near.start()
    for n, (part, dz, dx, below, arrivals) in enumerate(EVENTS):
        zl, xs = (u + NZ - dz) % NZ, (x + NX - dx) % NX
        if n == int(len(EVENTS) * 0.35):
            t_across.wait_recv()
            t_pass.start()

        @pl.when(zl < 4)
        def _():
            for k in arrivals:
                rows = (k * ROWS, ROWS) if dz == 0 and dx == 0 else PARTS[part]
                here = vg_ref.at[zl * NX + xs, pl.ds(*rows)]
                pltpu.make_async_copy(here, here, v_recv.at[(zl * NX + xs) * 4 + k]).wait()
            for child in below:
                copy = v_copy(part, dz, dx, child)
                if (dz, dx, child) == LATE:
                    pl.when(jnp.logical_not(first_row))(copy.start)
                else:
                    copy.start()

        if n == 3:

            @pl.when(first_row)
            def _():
                pl.semaphore_wait(late_sem, 1)
                for event in EVENTS[:4]:
                    if LATE[2] in event[3]:
                        v_copy(event[0], *LATE).start()

    t_near.wait_recv()
    t_pass.wait_recv()
    most = jnp.float32(0)
    for s in range(SLABS):
        most = jnp.maximum(most, jnp.max(tg_ref[s, CAP:ROWS, :]))
    rounds_ref[0, 0] = (most.astype(jnp.int32) + (CAP - 1)) // CAP
    rounds_out = pltpu.make_async_copy(rounds_ref, rounds_hbm, in_sem.at[len(inputs)])
    rounds_out.start()
    row = lax.broadcasted_iota(jnp.int32, tg_ref.shape[1:], 0)
    parts = [jnp.where(row == CAP, 0.0, tg_ref[s]) for s in range(SLABS)]
    high, low = split(jnp.concatenate(parts, axis=0).T)
    left_ref[...] = jnp.concatenate([high, high, low], axis=1)
    labels = ij_ref[...].astype(F32)
    mask_ref[...] = jnp.broadcast_to(labels, (128, labels.shape[1])).T

    rounds_out.wait()
    for copy in (t_across, t_near, t_pass):
        copy.wait_send()
    for k in range(2):
        here = mine & (y_lo == k)

        @pl.when(jnp.logical_not(here))
        def _():
            pltpu.make_async_remote_copy(
                src_ref=vc_ref,
                dst_ref=vg_ref.at[block, pl.ds(vir * ROWS, ROWS)],
                send_sem=y_send.at[k],
                recv_sem=v_recv.at[block * 4 + vir],
                device_id=(at(k, z, x), 2 * y_lo + z // 4),
                device_id_type=MESH,
            ).wait_send()

    for dz in range(NZ):

        @pl.when((u + NZ - dz) % NZ < 4)
        def _():
            for part in range(len(PARTS)):
                wait_all(part, SENT[part][dz], v_send.at[dz * len(PARTS) + part])

    def row_complete(zl):
        for dz in range(NZ):

            @pl.when((zl + dz) % NZ == u)
            def _():
                for part in range(len(PARTS)):
                    leaves = sum(LEAVES[part][4 * dz : 4 * dz + 4])
                    wait_all(part, leaves, leaf_recv.at[zl * len(PARTS) + part])

    for j in range(4):
        row_complete((row_order(u) // 4**j) % 4)


def spread(round_index, t, v, ij, cd, ab):
    n_ij, n_cd = t.shape
    anywhere = pl.BlockSpec(memory_space=pl.ANY)
    vmem = pl.BlockSpec(memory_space=pltpu.VMEM)
    return pl.pallas_call(
        spread_kernel,
        out_shape=(
            jax.ShapeDtypeStruct((16, SLABS * ROWS, v.shape[1]), F32),
            jax.ShapeDtypeStruct((n_ij, 3 * SLABS * ROWS), BF16),
            jax.ShapeDtypeStruct((n_ij, 128), F32),
            jax.ShapeDtypeStruct((1, 1), jnp.int32),
        ),
        in_specs=[anywhere] * 6,
        out_specs=(vmem, vmem, vmem, anywhere),
        scratch_shapes=[
            pltpu.VMEM(round_index.shape, jnp.int32),
            pltpu.VMEM(t.shape, F32),
            pltpu.VMEM(v.shape, F32),
            pltpu.VMEM((1, n_ij), jnp.int32),
            pltpu.VMEM((1, n_cd), jnp.int32),
            pltpu.VMEM((1, v.shape[1]), jnp.int32),
            pltpu.SMEM((1, 1), jnp.int32),
            pltpu.VMEM((ROWS, v.shape[1]), F32),
            pltpu.VMEM((SLABS, ROWS, n_ij), F32),
            pltpu.VMEM((G * ROWS, 2 * n_cd), BF16),
            pltpu.SemaphoreType.DMA((NZ * len(PARTS),)),
            pltpu.SemaphoreType.DMA((16 * len(PARTS),)),
            pltpu.SemaphoreType.DMA((4 * len(PARTS),)),
            pltpu.SemaphoreType.DMA((2,)),
            pltpu.SemaphoreType.DMA((3,)),
            pltpu.SemaphoreType.DMA((3,)),
            pltpu.SemaphoreType.DMA((7,)),
            pltpu.SemaphoreType.REGULAR,
        ],
        compiler_params=pltpu.CompilerParams(
            collective_id=0, has_side_effects=True, vmem_limit_bytes=32 << 20
        ),
        name="spread",
    )(round_index, t, v, ij[None, :], cd[None, :], ab[None, :])


def product_kernel(left_ref, vg_ref, mask_ref, out_hbm, out_buf, out_sem):
    copies = []
    width = out_buf.shape[2]
    for zl in range(4):
        out_buf[zl] = row_product(left_ref, vg_ref, mask_ref, zl)
        columns = pl.ds(zl * width, width)
        copy = pltpu.make_async_copy(out_buf.at[zl], out_hbm.at[:, columns], out_sem.at[zl])
        copy.start()
        copies.append(copy)
    for copy in copies:
        copy.wait()


def product(left, vg, mask):
    n_ij, width = left.shape[0], NX * vg.shape[2]
    vmem = pl.BlockSpec(memory_space=pltpu.VMEM)
    return pl.pallas_call(
        product_kernel,
        out_shape=jax.ShapeDtypeStruct((n_ij, 4 * width), F32),
        in_specs=[vmem] * 3,
        out_specs=pl.BlockSpec(memory_space=pl.ANY),
        scratch_shapes=[pltpu.VMEM((4, n_ij, width), F32), pltpu.SemaphoreType.DMA((4,))],
        compiler_params=pltpu.CompilerParams(vmem_limit_bytes=24 << 20),
        name="product",
    )(left, vg, mask)


def per_device(*args):
    def one_round(index):
        vg, left, mask, rounds = spread(jnp.full((1, 128), index), *args)
        return product(left, vg, mask), rounds

    ladder, rounds = one_round(jnp.int32(0))

    def more(state):
        return state[0] < rounds[0, 0]

    def next_round(state):
        index, total = state
        return index + 1, total + one_round(index)[0]

    return lax.while_loop(more, next_round, (jnp.int32(1), ladder))[1]


def solution(mesh):
    in_specs = (P("occ", "vir"), P("vir", "occ"), P("occ"), P("vir"), P("occ"))
    out_specs = P("occ", "vir")
    return jax.shard_map(
        per_device, mesh=mesh, in_specs=in_specs, out_specs=out_specs, check_vma=False
    )
```

```python
import functools

import jax
import jax.numpy as jnp
from jax import lax
from jax.experimental import pallas as pl
from jax.experimental.pallas import tpu as pltpu
from jax.sharding import PartitionSpec as P

MESH = pl.DeviceIdType.MESH
G = 8
CAP = 95
ROWS = CAP + 1
NX, NZ = 4, 8
F32, BF16 = jnp.float32, jnp.bfloat16


def split(value):
    high = value.astype(BF16)
    return high, (value - high.astype(F32)).astype(BF16)


def picker(round_index, labels):
    n_cd = labels.shape[1]
    member = lax.broadcasted_iota(jnp.int32, (G, n_cd), 0) == labels
    before = lax.broadcasted_iota(jnp.int32, (n_cd, n_cd), 0) < lax.broadcasted_iota(
        jnp.int32, (n_cd, n_cd), 1
    )
    below = jnp.dot(member.astype(BF16), before.astype(BF16), preferred_element_type=F32)
    rank = jnp.sum(jnp.where(member, below, 0.0), axis=0, keepdims=True).astype(jnp.int32)
    most = jnp.max(jnp.sum(member.astype(F32), axis=1, keepdims=True), axis=0, keepdims=True)
    place = rank - CAP * round_index
    slot = jnp.where((place >= 0) & (place < CAP), labels * ROWS + place, -1)
    pick = (lax.broadcasted_iota(jnp.int32, (G * ROWS, n_cd), 0) == slot).astype(BF16)
    return jnp.concatenate([pick, pick], axis=1), most


def compacted(pick2, both, dims, column_labels, last_row):
    wide = lax.dot_general(pick2, both, (dims, ((), ())), preferred_element_type=F32)
    out = jnp.zeros((ROWS, wide.shape[1]), F32)
    for g in range(G):
        out = jnp.where(column_labels == g, wide[g * ROWS : (g + 1) * ROWS], out)
    row = lax.broadcasted_iota(jnp.int32, out.shape, 0)
    return jnp.where(row == CAP, last_row, out)


SLABS = 4
PARTS = ((0, 80), (80, 80), (160, 112), (272, 112))
PARENTS = (
    (-1, 0, 1, 0, 0, 1, 2, 3, 4, 5, 6, 7, 8, 9, 10, 11,
     12, 13, 14, 15, 24, 25, 26, 27, 28, 29, 30, 31, 0, 1, 2, 3),
    (-1, 0, 3, 0, 0, 1, 2, 3, 4, 5, 6, 7, 8, 9, 10, 11,
     20, 21, 22, 23, 24, 25, 26, 27, 28, 29, 30, 31, 0, 1, 2, 3),
    (-1, 0, 1, 0, 0, 4, 5, 4, 4, 8, 9, 8, 8, 12, 13, 12,
     12, 16, 17, 16, 24, 20, 21, 20, 28, 24, 25, 24, 0, 28, 29, 28),
    (-1, 0, 3, 0, 0, 4, 7, 4, 4, 8, 11, 8, 8, 12, 15, 12,
     20, 16, 19, 16, 24, 20, 23, 20, 28, 24, 27, 24, 0, 28, 31, 28),
)
ORDER = (
    0, 32, 64, 96, 1, 33, 3, 35, 68, 100, 92, 124, 65, 97, 67, 99, 4, 36, 28, 60, 2, 34, 72, 104,
    88, 120, 5, 37, 69, 101, 7, 39, 71, 103, 29, 61, 93, 125, 31, 63, 95, 127, 66, 98, 8, 40, 24,
    56, 76, 108, 84, 116, 6, 38, 73, 105, 75, 107, 89, 121, 91, 123, 30, 62, 70, 102, 9, 41, 11,
    43, 25, 57, 27, 59, 94, 126, 12, 44, 20, 52, 80, 112, 77, 109, 79, 111, 85, 117, 87, 119, 10,
    42, 74, 106, 26, 58, 90, 122, 13, 45, 15, 47, 21, 53, 23, 55, 16, 48, 81, 113, 83, 115, 78,
    110, 86, 118, 14, 46, 22, 54, 17, 49, 19, 51, 82, 114, 18, 50,
)


def spread_plan():
    events, seen = [], set()
    children = [[[] for _ in range(32)] for _ in PARTS]
    for part, parents in enumerate(PARENTS):
        for child, parent in enumerate(parents):
            if parent >= 0:
                children[part][parent].append(child)

    def height(part, node):
        return max([1 + height(part, c) for c in children[part][node]], default=0)

    for item in ORDER:
        part, node = item // 32, item % 32
        below = sorted(children[part][node], key=lambda c: -height(part, c))
        if node:
            arrivals = [part]
        else:
            start, size = PARTS[part]
            spans = range(start // ROWS, (start + size - 1) // ROWS + 1)
            arrivals = [slab for slab in spans if slab not in seen]
            seen.update(arrivals)
        if below:
            events.append((part, node // 4, node % 4, below, arrivals))
    leaves = [[not c for c in nodes] for nodes in children]
    return events, leaves


EVENTS, LEAVES = spread_plan()
LATE = (0, 0, 4 * (NZ - 1))


SENT = [
    [sum(len(e[3]) for e in EVENTS if e[:2] == (part, dz)) for dz in range(NZ)]
    for part in range(len(PARTS))
]


STEPS = {}
for _part, _dz, _dx, _below, _ in EVENTS:
    for _c in _below:
        _step = ((_c // 4 - _dz) % NZ, (_c % 4 - _dx) % NX)
        STEPS.setdefault(_step, set()).update((_dz + zl) % NZ for zl in range(4))


def among(u, values):
    return functools.reduce(jnp.logical_or, [u == v for v in sorted(values)])


def row_product(left_ref, vg_ref, mask_ref, zl):
    blocks = [zl * NX + b for b in range(NX)]
    value = jnp.concatenate([vg_ref[b] for b in blocks], axis=1)
    labels = jnp.concatenate([vg_ref[b, CAP:ROWS, :] for b in blocks], axis=1)
    high, low = split(value)
    right = jnp.concatenate([high, low, high], axis=0)
    total = jnp.dot(left_ref[...], right, preferred_element_type=F32)
    return jnp.where(jnp.concatenate([mask_ref[...]] * NX, axis=1) == labels, total, 0.0)


def spread_kernel(
    round_hbm, t_hbm, v_hbm, ij_hbm, cd_hbm, ab_hbm, vg_ref, left_ref, mask_ref, rounds_hbm,
    round_ref, t_buf, v_buf, ij_ref, cd_ref, ab_ref, rounds_ref, vc_ref, tg_ref, pick_ref, v_send, v_recv, leaf_recv, y_send, t_send, t_recv, in_sem, late_sem,
):
    inputs = (cd_hbm, cd_ref), (round_hbm, round_ref), (v_hbm, v_buf), (ab_hbm, ab_ref)
    inputs += (t_hbm, t_buf), (ij_hbm, ij_ref)
    copies_in = [pltpu.make_async_copy(*pair, in_sem.at[k]) for k, pair in enumerate(inputs)]
    cd_in, round_in, v_in, ab_in, t_in, ij_in = copies_in
    for copy in copies_in:
        copy.start()
    occ, vir = lax.axis_index("occ"), lax.axis_index("vir")
    y_lo, z, x = occ // (NX * NZ), (occ // NX) % NZ, occ % NX
    y_hi, core = vir // 2, vir % 2
    u = (z + NZ - 4 * core) % NZ

    def at(y, z, x):
        return y * (NX * NZ) + z * NX + x

    def away(dz, dx):
        return (at(y_lo, (z + NZ + dz) % NZ, (x + NX + dx) % NX), vir)

    owner = z // 4 == core
    mine = owner & (y_lo == y_hi)
    sibling, across = (occ, vir + 1 - 2 * core), (occ, (vir + 2) % 4)

    barrier = pltpu.get_barrier_semaphore()

    def ready_for(peer):
        pl.semaphore_signal(barrier, inc=1, device_id=peer, device_id_type=MESH)

    for peer in (sibling, across):
        ready_for(peer)
    heard = 4 - mine.astype(jnp.int32)
    first_row, last_row = (u == 0) & (core == 0), (u == 7) & (core == 0)
    pl.when(first_row)(lambda: ready_for(away(-1, 0)))
    heard += last_row.astype(jnp.int32) - first_row.astype(jnp.int32)
    for (dz, dx), senders in STEPS.items():
        takes = among((u + NZ - dz) % NZ, senders)
        if (dz, dx) == (NZ - 1, 0):
            takes = takes & jnp.logical_not(last_row)
        pl.when(takes)(lambda: ready_for(away(-dz, -dx)))
        heard += among(u, senders).astype(jnp.int32)
    for k in range(4):
        pl.when(owner & jnp.logical_not(mine & (vir == k)))(
            lambda: ready_for((at(y_hi, z, x), k))
        )

    cd_in.wait()
    round_in.wait()
    pick2, most = picker(round_ref[:, 0:1], cd_ref[...])
    pick_ref[...] = pick2
    ab_in.wait()
    ab = ab_ref[...]
    v_in.wait()
    both = jnp.concatenate(split(v_buf[...]), axis=0)
    vc_ref[...] = compacted(pick2, both, ((1,), (0,)), ab, ab.astype(F32))
    pl.semaphore_wait(barrier, heard)
    pl.when(last_row)(
        lambda: pl.semaphore_signal(late_sem, 1, device_id=away(1, 0), device_id_type=MESH)
    )

    block = (z % 4) * NX + x
    for k in (1, 0):
        target = (at(k, z, x), 2 * y_lo + z // 4)
        here = mine & (y_lo == k)

        @pl.when(here)
        def _():
            pltpu.make_async_copy(
                vc_ref, vg_ref.at[block, pl.ds(vir * ROWS, ROWS)], v_recv.at[block * 4 + vir]
            ).start()

        @pl.when(jnp.logical_not(here))
        def _():
            pltpu.make_async_remote_copy(
                src_ref=vc_ref,
                dst_ref=vg_ref.at[block, pl.ds(vir * ROWS, ROWS)],
                send_sem=y_send.at[k],
                recv_sem=v_recv.at[block * 4 + vir],
                device_id=target,
                device_id_type=MESH,
            ).start()

    def t_copy(k, src, slab, peer):
        return pltpu.make_async_remote_copy(
            src_ref=src,
            dst_ref=tg_ref.at[slab],
            send_sem=t_send.at[k],
            recv_sem=t_recv.at[k],
            device_id=peer,
            device_id_type=MESH,
        )

    far = (vir + 2) % 4
    t_across = t_copy(0, tg_ref.at[vir], vir, across)
    t_near = t_copy(1, tg_ref.at[vir], vir, sibling)
    t_pass = t_copy(2, tg_ref.at[far], far, sibling)
    t_in.wait()
    ij_in.wait()
    both = jnp.concatenate(split(t_buf[...]), axis=1)
    tg_ref[vir] = compacted(pick_ref[...], both, ((1,), (1,)), ij_ref[...], most)

    near = {step: away(*step) for step in STEPS}
    row_at = [(u + NZ - dz) % NZ for dz in range(NZ)]
    column_at = [(x + NX - dx) % NX for dx in range(NX)]

    def v_copy(part, dz, dx, child):
        zl, xs = row_at[dz], column_at[dx]
        here = vg_ref.at[zl * NX + xs, pl.ds(*PARTS[part])]
        leaf = LEAVES[part][child]
        return pltpu.make_async_remote_copy(
            src_ref=here,
            dst_ref=here,
            send_sem=v_send.at[dz * len(PARTS) + part],
            recv_sem=leaf_recv.at[zl] if leaf else v_recv.at[(zl * NX + xs) * 4 + part],
            device_id=near[(child // 4 - dz) % NZ, (child % 4 - dx) % NX],
            device_id_type=MESH,
        )

    def wait_all(part, count, sem):
        if count:
            here = vg_ref.at[pl.ds(0, count), pl.ds(*PARTS[part])]
            pltpu.make_async_copy(here, here, sem).wait()

    for n, (part, dz, dx, below, arrivals) in enumerate(EVENTS):
        zl, xs = row_at[dz], column_at[dx]
        if n == int(len(EVENTS) * 0.35):
            t_across.start()
            t_near.start()
        if n == int(len(EVENTS) * 0.75):
            t_across.wait_recv()
            t_pass.start()

        @pl.when(zl < 4)
        def _():
            for k in arrivals:
                rows = (k * ROWS, ROWS) if dz == 0 and dx == 0 else PARTS[part]
                here = vg_ref.at[zl * NX + xs, pl.ds(*rows)]
                pltpu.make_async_copy(here, here, v_recv.at[(zl * NX + xs) * 4 + k]).wait()
            for child in below:
                copy = v_copy(part, dz, dx, child)
                if (dz, dx, child) == LATE:
                    pl.when(jnp.logical_not(first_row))(copy.start)
                else:
                    copy.start()

        if n == 3:

            @pl.when(first_row)
            def _():
                pl.semaphore_wait(late_sem, 1)
                for event in EVENTS[:4]:
                    if LATE[2] in event[3]:
                        v_copy(event[0], *LATE).start()

    t_near.wait_recv()
    t_pass.wait_recv()
    most = jnp.float32(0)
    for s in range(SLABS):
        most = jnp.maximum(most, jnp.max(tg_ref[s, CAP:ROWS, :]))
    rounds_ref[0, 0] = (most.astype(jnp.int32) + (CAP - 1)) // CAP
    rounds_out = pltpu.make_async_copy(rounds_ref, rounds_hbm, in_sem.at[len(inputs)])
    rounds_out.start()
    row = lax.broadcasted_iota(jnp.int32, tg_ref.shape[1:], 0)
    parts = [jnp.where(row == CAP, 0.0, tg_ref[s]) for s in range(SLABS)]
    high, low = split(jnp.concatenate(parts, axis=0).T)
    left_ref[...] = jnp.concatenate([high, high, low], axis=1)
    labels = ij_ref[...].astype(F32)
    mask_ref[...] = jnp.broadcast_to(labels, (128, labels.shape[1])).T

    rounds_out.wait()
    for copy in (t_across, t_near, t_pass):
        copy.wait_send()
    for k in range(2):
        here = mine & (y_lo == k)

        @pl.when(jnp.logical_not(here))
        def _():
            pltpu.make_async_remote_copy(
                src_ref=vc_ref,
                dst_ref=vg_ref.at[block, pl.ds(vir * ROWS, ROWS)],
                send_sem=y_send.at[k],
                recv_sem=v_recv.at[block * 4 + vir],
                device_id=(at(k, z, x), 2 * y_lo + z // 4),
                device_id_type=MESH,
            ).wait_send()

    for dz in range(NZ):

        @pl.when(row_at[dz] < 4)
        def _():
            for part in range(len(PARTS)):
                wait_all(part, SENT[part][dz], v_send.at[dz * len(PARTS) + part])

    for dz in (0, 1, 7, 2, 6, 3, 5, 4):
        leaf_rows = sum(
            PARTS[part][1] * sum(LEAVES[part][4 * dz : 4 * dz + 4]) for part in range(len(PARTS))
        )

        @pl.when(row_at[dz] < 4)
        def _():
            here = vg_ref.at[pl.ds(0, 4), pl.ds(0, leaf_rows // 4)]
            pltpu.make_async_copy(here, here, leaf_recv.at[row_at[dz]]).wait()


def spread(round_index, t, v, ij, cd, ab):
    n_ij, n_cd = t.shape
    anywhere = pl.BlockSpec(memory_space=pl.ANY)
    vmem = pl.BlockSpec(memory_space=pltpu.VMEM)
    return pl.pallas_call(
        spread_kernel,
        out_shape=(
            jax.ShapeDtypeStruct((16, SLABS * ROWS, v.shape[1]), F32),
            jax.ShapeDtypeStruct((n_ij, 3 * SLABS * ROWS), BF16),
            jax.ShapeDtypeStruct((n_ij, 128), F32),
            jax.ShapeDtypeStruct((1, 1), jnp.int32),
        ),
        in_specs=[anywhere] * 6,
        out_specs=(vmem, vmem, vmem, anywhere),
        scratch_shapes=[
            pltpu.VMEM(round_index.shape, jnp.int32),
            pltpu.VMEM(t.shape, F32),
            pltpu.VMEM(v.shape, F32),
            pltpu.VMEM((1, n_ij), jnp.int32),
            pltpu.VMEM((1, n_cd), jnp.int32),
            pltpu.VMEM((1, v.shape[1]), jnp.int32),
            pltpu.SMEM((1, 1), jnp.int32),
            pltpu.VMEM((ROWS, v.shape[1]), F32),
            pltpu.VMEM((SLABS, ROWS, n_ij), F32),
            pltpu.VMEM((G * ROWS, 2 * n_cd), BF16),
            pltpu.SemaphoreType.DMA((NZ * len(PARTS),)),
            pltpu.SemaphoreType.DMA((16 * len(PARTS),)),
            pltpu.SemaphoreType.DMA((4,)),
            pltpu.SemaphoreType.DMA((2,)),
            pltpu.SemaphoreType.DMA((3,)),
            pltpu.SemaphoreType.DMA((3,)),
            pltpu.SemaphoreType.DMA((7,)),
            pltpu.SemaphoreType.REGULAR,
        ],
        compiler_params=pltpu.CompilerParams(
            collective_id=0, has_side_effects=True, vmem_limit_bytes=32 << 20
        ),
        name="spread",
    )(round_index, t, v, ij[None, :], cd[None, :], ab[None, :])


def product_kernel(left_ref, vg_ref, mask_ref, out_hbm, out_buf, out_sem):
    copies = []
    width = out_buf.shape[2]
    for zl in range(4):
        out_buf[zl] = row_product(left_ref, vg_ref, mask_ref, zl)
        columns = pl.ds(zl * width, width)
        copy = pltpu.make_async_copy(out_buf.at[zl], out_hbm.at[:, columns], out_sem.at[zl])
        copy.start()
        copies.append(copy)
    for copy in copies:
        copy.wait()


def product(left, vg, mask):
    n_ij, width = left.shape[0], NX * vg.shape[2]
    vmem = pl.BlockSpec(memory_space=pltpu.VMEM)
    return pl.pallas_call(
        product_kernel,
        out_shape=jax.ShapeDtypeStruct((n_ij, 4 * width), F32),
        in_specs=[vmem] * 3,
        out_specs=pl.BlockSpec(memory_space=pl.ANY),
        scratch_shapes=[pltpu.VMEM((4, n_ij, width), F32), pltpu.SemaphoreType.DMA((4,))],
        compiler_params=pltpu.CompilerParams(vmem_limit_bytes=24 << 20),
        name="product",
    )(left, vg, mask)


def per_device(*args):
    def one_round(index):
        vg, left, mask, rounds = spread(jnp.full((1, 128), index), *args)
        return product(left, vg, mask), rounds

    ladder, rounds = one_round(jnp.int32(0))

    def more(state):
        return state[0] < rounds[0, 0]

    def next_round(state):
        index, total = state
        return index + 1, total + one_round(index)[0]

    return lax.while_loop(more, next_round, (jnp.int32(1), ladder))[1]


def solution(mesh):
    in_specs = (P("occ", "vir"), P("vir", "occ"), P("occ"), P("vir"), P("occ"))
    out_specs = P("occ", "vir")
    return jax.shard_map(
        per_device, mesh=mesh, in_specs=in_specs, out_specs=out_specs, check_vma=False
    )
```

```python
import functools

import jax
import jax.numpy as jnp
from jax import lax
from jax.experimental import pallas as pl
from jax.experimental.pallas import tpu as pltpu
from jax.sharding import PartitionSpec as P

MESH = pl.DeviceIdType.MESH
G = 8
CAP = 95
ROWS = CAP + 1
NX, NZ = 4, 8
F32, BF16 = jnp.float32, jnp.bfloat16


def split(value):
    high = value.astype(BF16)
    return high, (value - high.astype(F32)).astype(BF16)


def picker(round_index, labels):
    n_cd = labels.shape[1]
    member = lax.broadcasted_iota(jnp.int32, (G, n_cd), 0) == labels
    before = lax.broadcasted_iota(jnp.int32, (n_cd, n_cd), 0) < lax.broadcasted_iota(
        jnp.int32, (n_cd, n_cd), 1
    )
    below = jnp.dot(member.astype(BF16), before.astype(BF16), preferred_element_type=F32)
    rank = jnp.sum(jnp.where(member, below, 0.0), axis=0, keepdims=True).astype(jnp.int32)
    most = jnp.max(jnp.sum(member.astype(F32), axis=1, keepdims=True), axis=0, keepdims=True)
    place = rank - CAP * round_index
    slot = jnp.where((place >= 0) & (place < CAP), labels * ROWS + place, -1)
    pick = (lax.broadcasted_iota(jnp.int32, (G * ROWS, n_cd), 0) == slot).astype(BF16)
    return jnp.concatenate([pick, pick], axis=1), most


def compacted(pick2, both, dims, column_labels, last_row):
    wide = lax.dot_general(pick2, both, (dims, ((), ())), preferred_element_type=F32)
    out = jnp.zeros((ROWS, wide.shape[1]), F32)
    for g in range(G):
        out = jnp.where(column_labels == g, wide[g * ROWS : (g + 1) * ROWS], out)
    row = lax.broadcasted_iota(jnp.int32, out.shape, 0)
    return jnp.where(row == CAP, last_row, out)


SLABS = 4
PARTS = ((0, 80), (80, 80), (160, 112), (272, 112))
PARENTS = (
    (-1, 0, 1, 0, 0, 1, 2, 3, 4, 5, 6, 7, 8, 9, 10, 11,
     12, 13, 14, 15, 24, 25, 26, 27, 28, 29, 30, 31, 0, 1, 2, 3),
    (-1, 0, 3, 0, 0, 1, 2, 3, 4, 5, 6, 7, 8, 9, 10, 11,
     20, 21, 22, 23, 24, 25, 26, 27, 28, 29, 30, 31, 0, 1, 2, 3),
    (-1, 0, 1, 0, 0, 4, 5, 4, 4, 8, 9, 8, 8, 12, 13, 12,
     12, 16, 17, 16, 24, 20, 21, 20, 28, 24, 25, 24, 0, 28, 29, 28),
    (-1, 0, 3, 0, 0, 4, 7, 4, 4, 8, 11, 8, 8, 12, 15, 12,
     20, 16, 19, 16, 24, 20, 23, 20, 28, 24, 27, 24, 0, 28, 31, 28),
)
ORDER = (
    0, 32, 64, 96, 1, 33, 3, 35, 68, 100, 92, 124, 65, 97, 67, 99, 4, 36, 28, 60, 2, 34, 72, 104,
    88, 120, 5, 37, 69, 101, 7, 39, 71, 103, 29, 61, 93, 125, 31, 63, 95, 127, 66, 98, 8, 40, 24,
    56, 76, 108, 84, 116, 6, 38, 73, 105, 75, 107, 89, 121, 91, 123, 30, 62, 70, 102, 9, 41, 11,
    43, 25, 57, 27, 59, 94, 126, 12, 44, 20, 52, 80, 112, 77, 109, 79, 111, 85, 117, 87, 119, 10,
    42, 74, 106, 26, 58, 90, 122, 13, 45, 15, 47, 21, 53, 23, 55, 16, 48, 81, 113, 83, 115, 78,
    110, 86, 118, 14, 46, 22, 54, 17, 49, 19, 51, 82, 114, 18, 50,
)


def spread_plan():
    events, seen = [], set()
    children = [[[] for _ in range(32)] for _ in PARTS]
    for part, parents in enumerate(PARENTS):
        for child, parent in enumerate(parents):
            if parent >= 0:
                children[part][parent].append(child)

    def height(part, node):
        return max([1 + height(part, c) for c in children[part][node]], default=0)

    for item in ORDER:
        part, node = item // 32, item % 32
        below = sorted(children[part][node], key=lambda c: -height(part, c))
        if node:
            arrivals = [part]
        else:
            start, size = PARTS[part]
            spans = range(start // ROWS, (start + size - 1) // ROWS + 1)
            arrivals = [slab for slab in spans if slab not in seen]
            seen.update(arrivals)
        if below:
            events.append((part, node // 4, node % 4, below, arrivals))
    leaves = [[not c for c in nodes] for nodes in children]
    return events, leaves


EVENTS, LEAVES = spread_plan()
LATE = (0, 0, 4 * (NZ - 1))


SENT = [
    [sum(len(e[3]) for e in EVENTS if e[:2] == (part, dz)) for dz in range(NZ)]
    for part in range(len(PARTS))
]


STEPS = {}
for _part, _dz, _dx, _below, _ in EVENTS:
    for _c in _below:
        _step = ((_c // 4 - _dz) % NZ, (_c % 4 - _dx) % NX)
        STEPS.setdefault(_step, set()).update((_dz + zl) % NZ for zl in range(4))


def among(u, values):
    return functools.reduce(jnp.logical_or, [u == v for v in sorted(values)])


def row_product(left_ref, vg_ref, mask_ref, zl):
    blocks = [zl * NX + b for b in range(NX)]
    value = jnp.concatenate([vg_ref[b] for b in blocks], axis=1)
    labels = jnp.concatenate([vg_ref[b, CAP:ROWS, :] for b in blocks], axis=1)
    high, low = split(value)
    right = jnp.concatenate([high, low, high], axis=0)
    total = jnp.dot(left_ref[...], right, preferred_element_type=F32)
    return jnp.where(jnp.concatenate([mask_ref[...]] * NX, axis=1) == labels, total, 0.0)


def spread_kernel(
    round_hbm, t_hbm, v_hbm, ij_hbm, cd_hbm, ab_hbm, vg_ref, left_ref, mask_ref, rounds_hbm,
    round_ref, t_buf, v_buf, ij_ref, cd_ref, ab_ref, rounds_ref, vc_ref, tg_ref, pick_ref, v_send, v_recv, leaf_recv, y_send, t_send, t_recv, in_sem, late_sem,
):
    inputs = (cd_hbm, cd_ref), (round_hbm, round_ref), (v_hbm, v_buf), (ab_hbm, ab_ref)
    inputs += (t_hbm, t_buf), (ij_hbm, ij_ref)
    copies_in = [pltpu.make_async_copy(*pair, in_sem.at[k]) for k, pair in enumerate(inputs)]
    cd_in, round_in, v_in, ab_in, t_in, ij_in = copies_in
    for copy in copies_in:
        copy.start()
    occ, vir = lax.axis_index("occ"), lax.axis_index("vir")
    y_lo, z, x = occ // (NX * NZ), (occ // NX) % NZ, occ % NX
    y_hi, core = vir // 2, vir % 2
    u = (z + NZ - 4 * core) % NZ

    def at(y, z, x):
        return y * (NX * NZ) + z * NX + x

    def away(dz, dx):
        return (at(y_lo, (z + NZ + dz) % NZ, (x + NX + dx) % NX), vir)

    owner = z // 4 == core
    mine = owner & (y_lo == y_hi)
    sibling, across = (occ, vir + 1 - 2 * core), (occ, (vir + 2) % 4)

    barrier = pltpu.get_barrier_semaphore()

    def ready_for(peer):
        pl.semaphore_signal(barrier, inc=1, device_id=peer, device_id_type=MESH)

    for peer in (sibling, across):
        ready_for(peer)
    heard = 4 - mine.astype(jnp.int32)
    first_row, last_row = (u == 0) & (core == 0), (u == 7) & (core == 0)
    pl.when(first_row)(lambda: ready_for(away(-1, 0)))
    heard += last_row.astype(jnp.int32) - first_row.astype(jnp.int32)
    for (dz, dx), senders in STEPS.items():
        takes = among((u + NZ - dz) % NZ, senders)
        if (dz, dx) == (NZ - 1, 0):
            takes = takes & jnp.logical_not(last_row)
        pl.when(takes)(lambda: ready_for(away(-dz, -dx)))
        heard += among(u, senders).astype(jnp.int32)
    for k in range(4):
        pl.when(owner & jnp.logical_not(mine & (vir == k)))(
            lambda: ready_for((at(y_hi, z, x), k))
        )

    cd_in.wait()
    round_in.wait()
    pick2, most = picker(round_ref[:, 0:1], cd_ref[...])
    pick_ref[...] = pick2
    ab_in.wait()
    ab = ab_ref[...]
    v_in.wait()
    both = jnp.concatenate(split(v_buf[...]), axis=0)
    vc_ref[...] = compacted(pick2, both, ((1,), (0,)), ab, ab.astype(F32))
    pl.semaphore_wait(barrier, heard)
    pl.when(last_row)(
        lambda: pl.semaphore_signal(late_sem, 1, device_id=away(1, 0), device_id_type=MESH)
    )

    block = (z % 4) * NX + x
    for k in (1, 0):
        target = (at(k, z, x), 2 * y_lo + z // 4)
        here = mine & (y_lo == k)

        @pl.when(here)
        def _():
            pltpu.make_async_copy(
                vc_ref, vg_ref.at[block, pl.ds(vir * ROWS, ROWS)], v_recv.at[block * 4 + vir]
            ).start()

        @pl.when(jnp.logical_not(here))
        def _():
            pltpu.make_async_remote_copy(
                src_ref=vc_ref,
                dst_ref=vg_ref.at[block, pl.ds(vir * ROWS, ROWS)],
                send_sem=y_send.at[k],
                recv_sem=v_recv.at[block * 4 + vir],
                device_id=target,
                device_id_type=MESH,
            ).start()

    def t_copy(k, src, slab, peer):
        return pltpu.make_async_remote_copy(
            src_ref=src,
            dst_ref=tg_ref.at[slab],
            send_sem=t_send.at[k],
            recv_sem=t_recv.at[k],
            device_id=peer,
            device_id_type=MESH,
        )

    far = (vir + 2) % 4
    t_across = t_copy(0, tg_ref.at[vir], vir, across)
    t_near = t_copy(1, tg_ref.at[vir], vir, sibling)
    t_pass = t_copy(2, tg_ref.at[far], far, sibling)
    near = {step: away(*step) for step in STEPS}
    row_at = [(u + NZ - dz) % NZ for dz in range(NZ)]
    column_at = [(x + NX - dx) % NX for dx in range(NX)]

    def v_copy(part, dz, dx, child):
        zl, xs = row_at[dz], column_at[dx]
        here = vg_ref.at[zl * NX + xs, pl.ds(*PARTS[part])]
        leaf = LEAVES[part][child]
        return pltpu.make_async_remote_copy(
            src_ref=here,
            dst_ref=here,
            send_sem=v_send.at[dz * len(PARTS) + part],
            recv_sem=leaf_recv.at[zl] if leaf else v_recv.at[(zl * NX + xs) * 4 + part],
            device_id=near[(child // 4 - dz) % NZ, (child % 4 - dx) % NX],
            device_id_type=MESH,
        )

    def wait_all(part, count, sem):
        if count:
            here = vg_ref.at[pl.ds(0, count), pl.ds(*PARTS[part])]
            pltpu.make_async_copy(here, here, sem).wait()

    for n, (part, dz, dx, below, arrivals) in enumerate(EVENTS):
        zl, xs = row_at[dz], column_at[dx]
        if n == 4:
            t_in.wait()
            ij_in.wait()
            both = jnp.concatenate(split(t_buf[...]), axis=1)
            tg_ref[vir] = compacted(pick_ref[...], both, ((1,), (1,)), ij_ref[...], most)
        if n == int(len(EVENTS) * 0.35):
            t_across.start()
            t_near.start()
        if n == int(len(EVENTS) * 0.75):
            t_across.wait_recv()
            t_pass.start()

        @pl.when(zl < 4)
        def _():
            for k in arrivals:
                rows = (k * ROWS, ROWS) if dz == 0 and dx == 0 else PARTS[part]
                here = vg_ref.at[zl * NX + xs, pl.ds(*rows)]
                pltpu.make_async_copy(here, here, v_recv.at[(zl * NX + xs) * 4 + k]).wait()
            for child in below:
                copy = v_copy(part, dz, dx, child)
                if (dz, dx, child) == LATE:
                    pl.when(jnp.logical_not(first_row))(copy.start)
                else:
                    copy.start()

        if n == 3:

            @pl.when(first_row)
            def _():
                pl.semaphore_wait(late_sem, 1)
                for event in EVENTS[:4]:
                    if LATE[2] in event[3]:
                        v_copy(event[0], *LATE).start()

    t_near.wait_recv()
    t_pass.wait_recv()
    most = jnp.float32(0)
    for s in range(SLABS):
        most = jnp.maximum(most, jnp.max(tg_ref[s, CAP:ROWS, :]))
    rounds_ref[0, 0] = (most.astype(jnp.int32) + (CAP - 1)) // CAP
    rounds_out = pltpu.make_async_copy(rounds_ref, rounds_hbm, in_sem.at[len(inputs)])
    rounds_out.start()
    row = lax.broadcasted_iota(jnp.int32, tg_ref.shape[1:], 0)
    parts = [jnp.where(row == CAP, 0.0, tg_ref[s]) for s in range(SLABS)]
    high, low = split(jnp.concatenate(parts, axis=0).T)
    left_ref[...] = jnp.concatenate([high, high, low], axis=1)
    labels = ij_ref[...].astype(F32)
    mask_ref[...] = jnp.broadcast_to(labels, (128, labels.shape[1])).T

    rounds_out.wait()
    for copy in (t_across, t_near, t_pass):
        copy.wait_send()
    for k in range(2):
        here = mine & (y_lo == k)

        @pl.when(jnp.logical_not(here))
        def _():
            pltpu.make_async_remote_copy(
                src_ref=vc_ref,
                dst_ref=vg_ref.at[block, pl.ds(vir * ROWS, ROWS)],
                send_sem=y_send.at[k],
                recv_sem=v_recv.at[block * 4 + vir],
                device_id=(at(k, z, x), 2 * y_lo + z // 4),
                device_id_type=MESH,
            ).wait_send()

    for dz in range(NZ):

        @pl.when(row_at[dz] < 4)
        def _():
            for part in range(len(PARTS)):
                wait_all(part, SENT[part][dz], v_send.at[dz * len(PARTS) + part])

    for dz in (0, 1, 7, 2, 6, 3, 5, 4):
        leaf_rows = sum(
            PARTS[part][1] * sum(LEAVES[part][4 * dz : 4 * dz + 4]) for part in range(len(PARTS))
        )

        @pl.when(row_at[dz] < 4)
        def _():
            here = vg_ref.at[pl.ds(0, 4), pl.ds(0, leaf_rows // 4)]
            pltpu.make_async_copy(here, here, leaf_recv.at[row_at[dz]]).wait()


def spread(round_index, t, v, ij, cd, ab):
    n_ij, n_cd = t.shape
    anywhere = pl.BlockSpec(memory_space=pl.ANY)
    vmem = pl.BlockSpec(memory_space=pltpu.VMEM)
    return pl.pallas_call(
        spread_kernel,
        out_shape=(
            jax.ShapeDtypeStruct((16, SLABS * ROWS, v.shape[1]), F32),
            jax.ShapeDtypeStruct((n_ij, 3 * SLABS * ROWS), BF16),
            jax.ShapeDtypeStruct((n_ij, 128), F32),
            jax.ShapeDtypeStruct((1, 1), jnp.int32),
        ),
        in_specs=[anywhere] * 6,
        out_specs=(vmem, vmem, vmem, anywhere),
        scratch_shapes=[
            pltpu.VMEM(round_index.shape, jnp.int32),
            pltpu.VMEM(t.shape, F32),
            pltpu.VMEM(v.shape, F32),
            pltpu.VMEM((1, n_ij), jnp.int32),
            pltpu.VMEM((1, n_cd), jnp.int32),
            pltpu.VMEM((1, v.shape[1]), jnp.int32),
            pltpu.SMEM((1, 1), jnp.int32),
            pltpu.VMEM((ROWS, v.shape[1]), F32),
            pltpu.VMEM((SLABS, ROWS, n_ij), F32),
            pltpu.VMEM((G * ROWS, 2 * n_cd), BF16),
            pltpu.SemaphoreType.DMA((NZ * len(PARTS),)),
            pltpu.SemaphoreType.DMA((16 * len(PARTS),)),
            pltpu.SemaphoreType.DMA((4,)),
            pltpu.SemaphoreType.DMA((2,)),
            pltpu.SemaphoreType.DMA((3,)),
            pltpu.SemaphoreType.DMA((3,)),
            pltpu.SemaphoreType.DMA((7,)),
            pltpu.SemaphoreType.REGULAR,
        ],
        compiler_params=pltpu.CompilerParams(
            collective_id=0, has_side_effects=True, vmem_limit_bytes=32 << 20
        ),
        name="spread",
    )(round_index, t, v, ij[None, :], cd[None, :], ab[None, :])


def product_kernel(left_ref, vg_ref, mask_ref, out_hbm, out_buf, out_sem):
    copies = []
    width = out_buf.shape[2]
    for zl in range(4):
        out_buf[zl] = row_product(left_ref, vg_ref, mask_ref, zl)
        columns = pl.ds(zl * width, width)
        copy = pltpu.make_async_copy(out_buf.at[zl], out_hbm.at[:, columns], out_sem.at[zl])
        copy.start()
        copies.append(copy)
    for copy in copies:
        copy.wait()


def product(left, vg, mask):
    n_ij, width = left.shape[0], NX * vg.shape[2]
    vmem = pl.BlockSpec(memory_space=pltpu.VMEM)
    return pl.pallas_call(
        product_kernel,
        out_shape=jax.ShapeDtypeStruct((n_ij, 4 * width), F32),
        in_specs=[vmem] * 3,
        out_specs=pl.BlockSpec(memory_space=pl.ANY),
        scratch_shapes=[pltpu.VMEM((4, n_ij, width), F32), pltpu.SemaphoreType.DMA((4,))],
        compiler_params=pltpu.CompilerParams(vmem_limit_bytes=24 << 20),
        name="product",
    )(left, vg, mask)


def per_device(*args):
    def one_round(index):
        vg, left, mask, rounds = spread(jnp.full((1, 128), index), *args)
        return product(left, vg, mask), rounds

    ladder, rounds = one_round(jnp.int32(0))

    def more(state):
        return state[0] < rounds[0, 0]

    def next_round(state):
        index, total = state
        return index + 1, total + one_round(index)[0]

    return lax.while_loop(more, next_round, (jnp.int32(1), ladder))[1]


def solution(mesh):
    in_specs = (P("occ", "vir"), P("vir", "occ"), P("occ"), P("vir"), P("occ"))
    out_specs = P("occ", "vir")
    return jax.shard_map(
        per_device, mesh=mesh, in_specs=in_specs, out_specs=out_specs, check_vma=False
    )
```
